32 devices in a mesh: fsdp: 16 (over z, y, core), dp: 2 (over x).
Axes of the slice: x: 2, y: 2, z: 4, core: 2. Of those that a mesh axis runs over, the one named last changes fastest.
Arguments:
- tokens: bfloat16 [32, 1024, 1024], P(('fsdp', 'dp')), may hold values from -6 to 6
- segments: int32 [32, 1024], P(('fsdp', 'dp')), may hold values from 0 to 4, never falling along the last dimension, each value on 1 to 512 neighbouring positions
- cotangent: bfloat16 [32, 1024, 1024], P(('fsdp', 'dp')), may hold values from -6 to 6
- w_in: bfloat16 [1024, 3352], P(('fsdp', 'dp')), may hold values from -0.1875 to 0.1875
- w_out: bfloat16 [1536, 1024], P(None, ('fsdp', 'dp')), may hold values from -0.15625 to 0.15625
- w_query: bfloat16 [1024, 1024], P(('fsdp', 'dp')), may hold values from -0.1875 to 0.1875
- w_key: bfloat16 [1024, 256], P(('fsdp', 'dp')), may hold values from -0.1875 to 0.1875
- w_value: bfloat16 [1024, 256], P(('fsdp', 'dp')), may hold values from -0.1875 to 0.1875
- w_attn_out: bfloat16 [1024, 1024], P(None, ('fsdp', 'dp')), may hold values from -3 to 3
- w_gate: bfloat16 [1024, 2048], P(('fsdp', 'dp')), may hold values from -0.1875 to 0.1875
- w_up: bfloat16 [1024, 2048], P(('fsdp', 'dp')), may hold values from -0.1875 to 0.1875
- w_down: bfloat16 [2048, 1024], P(None, ('fsdp', 'dp')), may hold values from -0.125 to 0.125
- norm_in: float32 [1024], replicated, may hold values from 0.5 to 1.5
- conv_weight: float32 [4, 1792], replicated, may hold values from -3 to 3
- conv_bias: float32 [1792], replicated, may hold values from -3 to 3
- dt_bias: float32 [24], replicated, may hold values from -6 to -2
- a_log: float32 [24], replicated, may hold values from -4 to 1.5
- skip_gain: float32 [24], replicated, may hold values from 0.5 to 2
- norm_gated: float32 [1536], replicated, may hold values from 0.5 to 1.5
- norm_mid: float32 [1024], replicated, may hold values from 0.5 to 1.5
Outputs:
- mixed: bfloat16 [32, 1024, 1024], P(('fsdp', 'dp'))
- grad_tokens: float32 [32, 1024, 1024], P(('fsdp', 'dp'))
- grad_w_in: float32 [1024, 3352], P(('fsdp', 'dp'))
- grad_w_out: float32 [1536, 1024], P(None, ('fsdp', 'dp'))
- grad_w_query: float32 [1024, 1024], P(('fsdp', 'dp'))
- grad_w_key: float32 [1024, 256], P(('fsdp', 'dp'))
- grad_w_value: float32 [1024, 256], P(('fsdp', 'dp'))
- grad_w_attn_out: float32 [1024, 1024], P(None, ('fsdp', 'dp'))
- grad_w_gate: float32 [1024, 2048], P(('fsdp', 'dp'))
- grad_w_up: float32 [1024, 2048], P(('fsdp', 'dp'))
- grad_w_down: float32 [2048, 1024], P(None, ('fsdp', 'dp'))
- grad_norm_in: float32 [1024], replicated
- grad_conv_weight: float32 [4, 1792], replicated
- grad_conv_bias: float32 [1792], replicated
- grad_dt_bias: float32 [24], replicated
- grad_a_log: float32 [24], replicated
- grad_skip_gain: float32 [24], replicated
- grad_norm_gated: float32 [1536], replicated
- grad_norm_mid: float32 [1024], replicated
The draws below stay inside these ranges and needn't reach their ends.
Inputs may be any that keep to these rules, and one draw needn't show every extreme that they name: `segments`: within a sequence the document numbers never fall; a document has at most 512 tokens, and some has exactly that many.
All inputs are finite; a program needn't handle non-finite values.
Results may differ from the reference program's by a relative error of at most 0.012.
Values may be sent and summed in bfloat16 or wider, within the bound.
No kernel may reach another device: no remote copies, remote signals or barrier semaphores. Data moves between devices by JAX's collectives and lax.ppermute only.
A program may use at most 384 MiB of HBM per device.

```python
import math
import jax
import jax.numpy as jnp
import numpy as np
from jax import lax

D = 1024
HEADS = 8
KV_HEADS = 2
HEAD_DIM = 128
M_HEADS = 24
M_HDIM = 64
STATE = 128
CONV = 4
FF = 2048
LEN = 1024
SPAN = 128
D_SSM = 1536
CONV_CH = 1792
PROJ = 3352
SEQS = 32


def block_levels(key, dims, pieces, smallest, top_value):
    level, own = 1.0, jax.random.fold_in(key, 6)
    for dim, shards_of in pieces:
        draws = jnp.exp(jax.random.uniform(jax.random.fold_in(own, dim), (shards_of,), jnp.float32, smallest / len(pieces), top_value / len(pieces)))
        level = level * jnp.repeat(draws, dims[dim] // shards_of).reshape([-1 if axis == dim else 1 for axis in range(len(dims))])
    return level


def split_up(number_of, total, reach, skew):
    weights = [(1 << 20) // math.isqrt(rank ** skew) + 1 for rank in range(2, number_of + 1)]
    surplus, given = total - reach - (number_of - 1), [1] * (number_of - 1)
    while surplus > 0:
        movable = [i for i in range(number_of - 1) if given[i] < reach]
        pool, remaining = sum([weights[i] for i in movable]), surplus
        for i in movable:
            more = min(reach - given[i], max(1, remaining * weights[i] // pool), surplus)
            given[i] = given[i] + more
            surplus = surplus - more
    return np.array([reach] + given)


def uneven(own_key, number_of, total, most, lean):
    if number_of == 2:
        one = jax.random.randint(own_key, (), max(1, total - most), min(most, total - 1) + 1)
        return jnp.stack([one, total - one])
    sizes = jnp.asarray(split_up(number_of, total, most, lean), jnp.int32)
    twos = (number_of - 1) // 2
    source_of, receiver = sizes[1:1 + 2 * twos:2], sizes[2:2 + 2 * twos:2]
    room = jnp.minimum(source_of - 1, most - receiver)
    passed = jax.random.randint(jax.random.fold_in(own_key, 1), (twos,), 0, 1 << 20) % (room + 1)
    sizes = sizes.at[1:1 + 2 * twos:2].set(source_of - passed).at[2:2 + 2 * twos:2].set(receiver + passed)
    return sizes[jax.random.permutation(jax.random.fold_in(own_key, 2), number_of)]


def normal_values(stream_key, shape, scale, bound, split=(), held_as=jnp.bfloat16):
    factor_of = block_levels(stream_key, shape, split, -0.22, 0.18) if split else 1.0
    drawn = jax.random.normal(stream_key, shape, jnp.float32) * scale * factor_of
    return jnp.minimum(jnp.maximum(drawn, -bound), bound).astype(held_as)


def setup_inputs(seed: int = 0) -> dict:
    streams_of = jax.random.split(jax.random.key(seed), 21)
    tokens = normal_values(streams_of[0], (SEQS, LEN, D), 1.0, 6.0, ((0, 32),))
    segments = jax.vmap(lambda own: jnp.searchsorted(jnp.cumsum(uneven(own, 5, LEN, LEN // 2, 0)), jnp.arange(LEN), side="right"))(jax.random.split(streams_of[1], SEQS)).reshape((SEQS, LEN)).astype(jnp.int32)
    cotangent = normal_values(streams_of[2], (SEQS, LEN, D), 1.0, 6.0, ((0, 32),))
    w_in = normal_values(streams_of[3], (D, PROJ), D ** -0.5, 0.1875, ((0, 32),))
    w_out = normal_values(streams_of[4], (D_SSM, D), D_SSM ** -0.5, 0.15625, ((1, 32),))
    w_query = normal_values(streams_of[5], (D, HEADS * HEAD_DIM), D ** -0.5, 0.1875, ((0, 32),))
    w_key = normal_values(streams_of[6], (D, KV_HEADS * HEAD_DIM), D ** -0.5, 0.1875, ((0, 32),))
    w_value = normal_values(streams_of[7], (D, KV_HEADS * HEAD_DIM), D ** -0.5, 0.1875, ((0, 32),))
    w_attn_out = normal_values(streams_of[8], (HEADS * HEAD_DIM, D), (D // 256) ** -0.5, 3.0, ((1, 32),))
    w_gate = normal_values(streams_of[9], (D, FF), D ** -0.5, 0.1875, ((0, 32),))
    w_up = normal_values(streams_of[10], (D, FF), D ** -0.5, 0.1875, ((0, 32),))
    w_down = normal_values(streams_of[11], (FF, D), FF ** -0.5, 0.125, ((1, 32),))
    norm_in = jnp.clip(1.0 + 0.1 * jax.random.normal(streams_of[12], (D,), jnp.float32), 0.5, 1.5)
    conv_weight = normal_values(streams_of[13], (CONV, CONV_CH), CONV ** -0.5, 3.0, (), jnp.float32)
    conv_bias = normal_values(streams_of[14], (CONV_CH,), 0.5, 3.0, (), jnp.float32)
    dt_bias = jnp.clip(jax.random.uniform(streams_of[15], (M_HEADS,), jnp.float32, -6.0, -2.0), -6.0, -2.0)
    a_log = jnp.clip(jax.random.uniform(streams_of[16], (M_HEADS,), jnp.float32, -4.0, 1.5), -4.0, 1.5)
    skip_gain = jnp.clip(jax.random.uniform(streams_of[17], (M_HEADS,), jnp.float32, 0.5, 2.0), 0.5, 2.0)
    norm_gated = jnp.clip(1.0 + 0.1 * jax.random.normal(streams_of[18], (D_SSM,), jnp.float32), 0.5, 1.5)
    norm_mid = jnp.clip(1.0 + 0.1 * jax.random.normal(streams_of[19], (D,), jnp.float32), 0.5, 1.5)
    return {"tokens": tokens, "segments": segments, "cotangent": cotangent, "w_in": w_in, "w_out": w_out, "w_query": w_query, "w_key": w_key, "w_value": w_value, "w_attn_out": w_attn_out, "w_gate": w_gate, "w_up": w_up, "w_down": w_down, "norm_in": norm_in, "conv_weight": conv_weight, "conv_bias": conv_bias, "dt_bias": dt_bias, "a_log": a_log, "skip_gain": skip_gain, "norm_gated": norm_gated, "norm_mid": norm_mid}


highest = lax.Precision.HIGHEST
eps = 1e-06
rope_base = 100000000000.0

@jax.custom_vjp
def low(v):
    return lax.optimization_barrier(v.astype(jnp.bfloat16)).astype(jnp.float32)

@jax.custom_vjp
def low_back(v):
    return v

def low_keep(v):
    return (low(v), None)

def low_pass(kept, grad):
    return (grad,)

def back_keep(v):
    return (v, None)

def back_low(kept, grad):
    return (low(grad),)
low.defvjp(low_keep, low_pass)
low_back.defvjp(back_keep, back_low)

def project(left_op, right_op):
    return jnp.dot(left_op, right_op, precision=highest)

def rms_norm(values, gain):
    return values * lax.rsqrt(lax.optimization_barrier(jnp.mean(values * values, axis=-1, keepdims=True)) + eps) * gain

def rotate(values, positions):
    half_dim = values.shape[-1] // 2
    frequency = rope_base ** (-jnp.arange(half_dim, dtype=jnp.float32) / half_dim)
    angles = positions.astype(jnp.float32)[:, None] * frequency[None, :]
    cosine = jnp.cos(angles)[:, None, :]
    sine = jnp.sin(angles)[:, None, :]
    front_half = values[..., :half_dim]
    back_half = values[..., half_dim:]
    return jnp.concatenate([front_half * cosine - back_half * sine, back_half * cosine + front_half * sine], axis=-1)

def conv_reset(conv_in, doc_ids, conv_weight, conv_bias):
    length = conv_in.shape[0]
    summed = conv_bias[None, :] + conv_weight[0][None, :] * conv_in
    for offset in range(1, conv_weight.shape[0]):
        shifted = jnp.pad(conv_in, ((offset, 0), (0, 0)))[:length]
        shifted_doc = jnp.pad(doc_ids, (offset, 0), constant_values=-1)[:length]
        summed = summed + jnp.where((shifted_doc == doc_ids)[:, None], conv_weight[offset][None, :] * shifted, 0.0)
    return summed

def scan_block(carried_in, block_in):
    ssm_state, prior_doc = carried_in
    x_block, b_block, c_block, step_block, decay_block, doc_block = block_in
    order = jnp.arange(doc_block.shape[0])
    cum_decay = jnp.cumsum(decay_block, axis=0)
    allowed = (doc_block[:, None] == doc_block[None, :]) & (order[:, None] >= order[None, :])
    log_gap = jnp.where(allowed[:, :, None], cum_decay[:, None, :] - cum_decay[None, :, :], 0.0)
    decays = jnp.where(allowed[:, :, None], jnp.exp(log_gap), 0.0)
    affinity = jnp.dot(c_block, b_block.T, precision=highest)
    weights = affinity[:, :, None] * decays * step_block[None, :, :]
    inside = jnp.einsum('tsh,shp->thp', weights, x_block, precision=highest)
    carried = jnp.where((doc_block == prior_doc)[:, None], jnp.exp(cum_decay), 0.0)
    from_state = jnp.einsum('tn,hpn->thp', c_block, ssm_state, precision=highest) * carried[:, :, None]
    last_doc = doc_block[-1]
    tail_decay = jnp.where((doc_block == last_doc)[:, None], jnp.exp(cum_decay[-1][None, :] - cum_decay), 0.0) * step_block
    keep_factor = jnp.where(last_doc == prior_doc, jnp.exp(cum_decay[-1]), 0.0)
    new_state = ssm_state * keep_factor[:, None, None] + jnp.einsum('shp,sn->hpn', x_block * tail_decay[:, :, None], b_block, precision=highest)
    return ((new_state, last_doc), inside + from_state)

def ssd_scan(x_heads, b_proj, c_proj, step_size, log_decay, doc_ids):
    blocks = x_heads.shape[0] // SPAN

    def shape_blocks(member):
        return member.reshape((blocks, SPAN) + member.shape[1:])
    start = (jnp.zeros((M_HEADS, M_HDIM, STATE), jnp.float32), jnp.array(-1, jnp.int32))
    members = tuple((shape_blocks(member) for member in (x_heads, b_proj, c_proj, step_size, log_decay, doc_ids)))
    final_carry, ssm_out = lax.scan(jax.checkpoint(scan_block), start, members)
    return ssm_out.reshape(x_heads.shape)

def attention(query, key, value, doc_ids):
    length = query.shape[0]
    block_rows = min(512, length)
    blocks = length // block_rows
    group_size = HEADS // KV_HEADS
    positions = jnp.arange(length)
    query_blocks = query.reshape(blocks, block_rows, KV_HEADS, group_size, HEAD_DIM)

    def attend_block(block_in):
        query_block, query_pos, query_doc = block_in
        scores = jnp.einsum('bgrd,kgd->bgrk', query_block, key, precision=highest) * HEAD_DIM ** (-0.5)
        allowed = (query_pos[:, None] >= positions[None, :]) & (query_doc[:, None] == doc_ids[None, :])
        scores = jnp.where(allowed[:, None, None, :], scores, -1e+30)
        row_max = lax.optimization_barrier(jnp.max(scores, axis=-1, keepdims=True))
        exponent = jnp.exp(scores - row_max)
        probability = low(exponent / lax.optimization_barrier(jnp.sum(exponent, axis=-1, keepdims=True)))
        return jnp.einsum('bgrk,kgd->bgrd', probability, value, precision=highest)
    result = lax.map(jax.checkpoint(attend_block), (query_blocks, positions.reshape(blocks, block_rows), doc_ids.reshape(blocks, block_rows)))
    return result.reshape(length, HEADS * HEAD_DIM)

def mixer_piece(doc_ids, stream, weights, small_params):
    w_in, w_out, w_query, w_key, w_value, w_attn_out = weights
    norm_in, conv_weight, conv_bias, dt_bias, a_log, skip_gain, norm_gated = small_params
    length = stream.shape[0]
    normed = low(rms_norm(stream, norm_in))
    mixer_proj = low_back(project(normed, w_in))
    z_gate = mixer_proj[:, :D_SSM]
    conv_in = mixer_proj[:, D_SSM:D_SSM + CONV_CH]
    dt_raw = mixer_proj[:, D_SSM + CONV_CH:]
    conv_act = jax.nn.silu(conv_reset(conv_in, doc_ids, conv_weight, conv_bias))
    x_heads = low(conv_act[:, :D_SSM]).reshape(length, M_HEADS, M_HDIM)
    b_proj = low(conv_act[:, D_SSM:D_SSM + STATE])
    c_proj = low(conv_act[:, D_SSM + STATE:])
    step_size = jax.nn.softplus(dt_raw + dt_bias)
    log_decay = -step_size * jnp.exp(a_log)
    ssm_out = ssd_scan(x_heads, b_proj, c_proj, step_size, log_decay, doc_ids) + skip_gain[None, :, None] * x_heads
    gated = rms_norm(ssm_out.reshape(length, D_SSM) * jax.nn.silu(z_gate), norm_gated)
    mamba_branch = low_back(project(low(gated), w_out))
    positions = jnp.arange(length)
    query = low(rotate(low_back(project(normed, w_query)).reshape(length, HEADS, HEAD_DIM), positions))
    key = low(rotate(low_back(project(normed, w_key)).reshape(length, KV_HEADS, HEAD_DIM), positions))
    value = low(low_back(project(normed, w_value))).reshape(length, KV_HEADS, HEAD_DIM)
    attended = attention(query, key, value, doc_ids)
    attn_branch = low_back(project(low(attended), w_attn_out))
    return stream + attn_branch + mamba_branch

def ffn_piece(resid, weights, norm_mid):
    w_gate, w_up, w_down = weights
    mid_in = low(rms_norm(resid, norm_mid))
    gate = low_back(project(mid_in, w_gate))
    up_proj = low_back(project(mid_in, w_up))
    hidden = low(jax.nn.silu(gate) * up_proj)
    return resid + low_back(project(hidden, w_down))

def reference(tokens, segments, cotangent, w_in, w_out, w_query, w_key, w_value, w_attn_out, w_gate, w_up, w_down, norm_in, conv_weight, conv_bias, dt_bias, a_log, skip_gain, norm_gated, norm_mid):
    params = tuple((member.astype(jnp.float32) for member in (w_in, w_out, w_query, w_key, w_value, w_attn_out, w_gate, w_up, w_down, norm_in, conv_weight, conv_bias, dt_bias, a_log, skip_gain, norm_gated, norm_mid)))

    def per_sequence(summed, sequence):
        stream, doc_ids, cot_seq = sequence

        def whole(stream_in, param_in):
            resid = mixer_piece(doc_ids, stream_in, param_in[:6], param_in[9:16])
            return ffn_piece(resid, param_in[6:9], param_in[16])
        block_out, backward = jax.vjp(whole, stream, params)
        grad_stream, grad_params = backward(cot_seq)
        summed = tuple((left_val + right_val for left_val, right_val in zip(summed, grad_params)))
        return (summed, (block_out.astype(jnp.bfloat16), grad_stream))
    zero_grads = tuple((jnp.zeros_like(member) for member in params))
    summed, (outputs, grad_tokens) = lax.scan(per_sequence, zero_grads, (tokens.astype(jnp.float32), segments, cotangent.astype(jnp.float32)))
    return (outputs, grad_tokens) + summed
```

```python
from functools import partial

import jax
import jax.numpy as jnp
from jax import lax
from jax.experimental import pallas as pl
from jax.experimental.pallas import tpu as pltpu
from jax.sharding import PartitionSpec as P

HEADS = 8
KV_HEADS = 2
HEAD_DIM = 128
M_HEADS = 24
M_HDIM = 64
STATE = 128
SPAN = 128
D_SSM = 1536
CONV_CH = 1792
QKV = (HEADS + 2 * KV_HEADS) * HEAD_DIM
PAIRS = M_HEADS // 2
QROWS = 256
REACH = 512

AXES = ("fsdp", "dp")
bf16 = jnp.bfloat16
f32 = jnp.float32
eps = 1e-06
rope_base = 100000000000.0
NEG = -1e30

NT = (((1,), (1,)), ((), ()))
TN = (((0,), (0,)), ((), ()))


def mm(left, right):
    return jnp.dot(left, right, preferred_element_type=f32)


def mm_nt(left, right):
    return lax.dot_general(left, right, NT, preferred_element_type=f32)


def mm_tn(left, right):
    return lax.dot_general(left, right, TN, preferred_element_type=f32)


def exact_mm(left, right):
    return jnp.dot(left, right, precision=lax.Precision.HIGHEST, preferred_element_type=f32)


def split_mm(value, selector):
    high = value.astype(bf16)
    low = (value - high.astype(f32)).astype(bf16)
    return mm(high, selector) + mm(low, selector)


def iota2(shape, axis):
    return lax.broadcasted_iota(jnp.int32, shape, axis)


def head_spread():
    rows = iota2((SPAN, D_SSM), 0)
    cols = iota2((SPAN, D_SSM), 1)
    return jnp.where(cols // M_HDIM == rows, 1.0, 0.0).astype(bf16)


def head_gather():
    rows = iota2((D_SSM, SPAN), 0)
    cols = iota2((D_SSM, SPAN), 1)
    return jnp.where(rows // M_HDIM == cols, 1.0, 0.0).astype(bf16)


def split_pair(block):
    lanes = iota2(block.shape, 1)
    zero = jnp.zeros_like(block)
    return jnp.concatenate(
        [jnp.where(lanes < M_HDIM, block, zero), jnp.where(lanes < M_HDIM, zero, block)], axis=0
    )


def block_terms(ld_ref, st_ref, spread):
    ld = ld_ref[...]
    st = st_ref[...]
    rows = iota2((SPAN, SPAN), 0)
    cols = iota2((SPAN, SPAN), 1)
    cum = exact_mm(jnp.where(rows >= cols, 1.0, 0.0), ld)
    cum_t = cum.T
    st_t = st.T
    doc = st[:, 127:128]
    prior = st[:, 126:127]
    last = st[:, 125:126]
    doc_row = st_t[127:128, :]
    carried = jnp.where(doc == prior, jnp.exp(cum), 0.0)
    gap = jnp.where(doc == last, jnp.exp(cum[SPAN - 1 : SPAN, :] - cum), 0.0)
    keep = jnp.where(last == prior, jnp.exp(cum[SPAN - 1 : SPAN, :]), 0.0)
    keep = keep[0:8, :]
    return (st, cum, cum_t, st_t, doc, doc_row, carried, gap, keep)


def scan_fwd_kernel(x_ref, b_ref, c_ref, ld_ref, st_ref, y_ref, states_ref, state):
    spread = head_spread()

    @pl.when(pl.program_id(0) == 0)
    def _():
        state[...] = jnp.zeros_like(state)

    st, cum, cum_t, st_t, doc, doc_row, carried, gap, keep = block_terms(ld_ref, st_ref, spread)
    rows = iota2((SPAN, SPAN), 0)
    cols = iota2((SPAN, SPAN), 1)
    bias = jnp.where((doc == doc_row) & (rows >= cols), 0.0, NEG)
    b_blk = b_ref[...]
    c_blk = c_ref[...]
    affinity = mm_nt(c_blk, b_blk)
    old = state[...]
    old_low = old.astype(bf16)
    states_ref[0] = old_low
    from_state = mm(c_blk, old_low) * split_mm(carried, spread)
    for pair in range(PAIRS):
        lo, hi = pair * SPAN, (pair + 1) * SPAN
        mats = []
        for h in (2 * pair, 2 * pair + 1):
            decay = jnp.exp(cum[:, h : h + 1] - cum_t[h : h + 1, :] + bias)
            mats.append((affinity * decay * st_t[h : h + 1, :]).astype(bf16))
        inside = mm(jnp.concatenate(mats, axis=1), split_pair(x_ref[:, lo:hi]))
        y_ref[:, lo:hi] = inside + from_state[:, lo:hi]
    tail = split_mm(gap * st, spread)
    pushed = (x_ref[...].astype(f32) * tail).astype(bf16)
    state[...] = old * split_mm(keep, spread)[0:1, :] + mm_tn(b_blk, pushed)


def scan_bwd_kernel(
    x_ref, b_ref, c_ref, ld_ref, st_ref, states_ref, dy_ref,
    dx_ref, db_ref, dc_ref, dst_ref, dld_ref, dstate, grow, gcol,
):
    spread = head_spread()
    gather = head_gather()

    @pl.when(pl.program_id(0) == 0)
    def _():
        dstate[...] = jnp.zeros_like(dstate)
        grow[...] = jnp.zeros_like(grow)
        gcol[...] = jnp.zeros_like(gcol)

    st, cum, cum_t, st_t, doc, doc_row, carried, gap, keep = block_terms(ld_ref, st_ref, spread)
    rows = iota2((SPAN, SPAN), 0)
    cols = iota2((SPAN, SPAN), 1)
    bias = jnp.where((doc == doc_row) & (cols >= rows), 0.0, NEG)
    b_blk = b_ref[...]
    c_blk = c_ref[...]
    x_blk = x_ref[...]
    dy = dy_ref[...]
    dy_low = dy.astype(bf16)
    affinity = mm_nt(b_blk, c_blk)
    old_low = states_ref[0]
    d_new = dstate[...]
    d_new_low = d_new.astype(bf16)
    carried_wide = split_mm(carried, spread)
    tail_wide = split_mm(gap * st, spread)
    keep_wide = split_mm(keep, spread)[0:1, :]
    from_tail = mm(b_blk, d_new_low)
    d_aff = jnp.zeros((SPAN, SPAN), f32)
    for pair in range(PAIRS):
        lo, hi = pair * SPAN, (pair + 1) * SPAN
        d_mats = mm_nt(split_pair(x_blk[:, lo:hi]), dy_low[:, lo:hi])
        mats = []
        for which, h in enumerate((2 * pair, 2 * pair + 1)):
            step = st[:, h : h + 1]
            decay = jnp.exp(cum_t[h : h + 1, :] - cum[:, h : h + 1] + bias)
            scaled = affinity * decay
            mats.append((scaled * step).astype(bf16))
            d_mat = d_mats[which * SPAN : (which + 1) * SPAN, :]
            d_aff = d_aff + d_mat * decay * step
            products = d_mat * scaled
            gcol[:, h : h + 1] = jnp.sum(products, axis=1, keepdims=True)
            grow[h : h + 1, :] = jnp.sum(products * step, axis=0, keepdims=True)
        inside = mm(jnp.concatenate(mats, axis=1), split_pair(dy_low[:, lo:hi]))
        dx_ref[:, lo:hi] = inside + from_tail[:, lo:hi] * tail_wide[:, lo:hi]
    flowing = dy * carried_wide
    flowing_low = flowing.astype(bf16)
    d_cum = split_mm(flowing * mm(c_blk, old_low), gather)
    d_tail = split_mm(x_blk.astype(f32) * from_tail, gather)
    moved = d_tail * gap * st
    d_keep = jnp.sum(d_new * old_low.astype(f32), axis=0, keepdims=True)
    d_keep = split_mm(jnp.broadcast_to(d_keep, (8, D_SSM)), gather) * keep
    at_end = jnp.sum(moved, axis=0, keepdims=True) + d_keep[0:1, :]
    d_cum = d_cum - moved + grow[...].T - gcol[...] * st
    d_cum = d_cum + jnp.where(rows == SPAN - 1, at_end, 0.0)
    dst_ref[...] = gcol[...] + d_tail * gap
    dld_ref[...] = exact_mm(jnp.where(cols >= rows, 1.0, 0.0), d_cum)
    d_aff_low = d_aff.astype(bf16)
    pushed = (x_blk.astype(f32) * tail_wide).astype(bf16)
    dc_ref[...] = mm_tn(d_aff_low, b_blk) + mm_nt(flowing_low, old_low)
    db_ref[...] = mm(d_aff_low, c_blk) + mm_nt(pushed, d_new_low)
    dstate[...] = d_new * keep_wide + mm_tn(c_blk, flowing_low)


def scan_fwd(act_low, ld, st):
    length = act_low.shape[0]
    blocks = length // SPAN
    return pl.pallas_call(
        scan_fwd_kernel,
        grid=(blocks,),
        in_specs=[
            pl.BlockSpec((SPAN, D_SSM), lambda i: (i, 0)),
            pl.BlockSpec((SPAN, STATE), lambda i: (i, D_SSM // STATE)),
            pl.BlockSpec((SPAN, STATE), lambda i: (i, D_SSM // STATE + 1)),
            pl.BlockSpec((SPAN, 128), lambda i: (i, 0)),
            pl.BlockSpec((SPAN, 128), lambda i: (i, 0)),
        ],
        out_specs=[
            pl.BlockSpec((SPAN, D_SSM), lambda i: (i, 0)),
            pl.BlockSpec((1, STATE, D_SSM), lambda i: (i, 0, 0)),
        ],
        out_shape=[
            jax.ShapeDtypeStruct((length, D_SSM), f32),
            jax.ShapeDtypeStruct((blocks, STATE, D_SSM), bf16),
        ],
        scratch_shapes=[pltpu.VMEM((STATE, D_SSM), f32)],
        compiler_params=pltpu.CompilerParams(vmem_limit_bytes=40 * 2**20),
    )(act_low, act_low, act_low, ld, st)


def scan_bwd(act_low, ld, st, states, dy):
    length = act_low.shape[0]
    blocks = length // SPAN
    end = blocks - 1
    return pl.pallas_call(
        scan_bwd_kernel,
        grid=(blocks,),
        in_specs=[
            pl.BlockSpec((SPAN, D_SSM), lambda i: (end - i, 0)),
            pl.BlockSpec((SPAN, STATE), lambda i: (end - i, D_SSM // STATE)),
            pl.BlockSpec((SPAN, STATE), lambda i: (end - i, D_SSM // STATE + 1)),
            pl.BlockSpec((SPAN, 128), lambda i: (end - i, 0)),
            pl.BlockSpec((SPAN, 128), lambda i: (end - i, 0)),
            pl.BlockSpec((1, STATE, D_SSM), lambda i: (end - i, 0, 0)),
            pl.BlockSpec((SPAN, D_SSM), lambda i: (end - i, 0)),
        ],
        out_specs=[
            pl.BlockSpec((SPAN, D_SSM), lambda i: (end - i, 0)),
            pl.BlockSpec((SPAN, STATE), lambda i: (end - i, 0)),
            pl.BlockSpec((SPAN, STATE), lambda i: (end - i, 0)),
            pl.BlockSpec((SPAN, 128), lambda i: (end - i, 0)),
            pl.BlockSpec((SPAN, 128), lambda i: (end - i, 0)),
        ],
        out_shape=[
            jax.ShapeDtypeStruct((length, D_SSM), f32),
            jax.ShapeDtypeStruct((length, STATE), f32),
            jax.ShapeDtypeStruct((length, STATE), f32),
            jax.ShapeDtypeStruct((length, 128), f32),
            jax.ShapeDtypeStruct((length, 128), f32),
        ],
        scratch_shapes=[
            pltpu.VMEM((STATE, D_SSM), f32),
            pltpu.VMEM((SPAN, SPAN), f32),
            pltpu.VMEM((SPAN, SPAN), f32),
        ],
        compiler_params=pltpu.CompilerParams(vmem_limit_bytes=40 * 2**20),
    )(act_low, act_low, act_low, ld, st, states, dy)


def key_span(block):
    return max(0, block * QROWS - REACH), (block + 1) * QROWS


def fill_bias(doc_col_ref, doc_row_ref, bias, blocks):
    for block in range(blocks):
        k0, k1 = key_span(block)
        q0, q1 = block * QROWS, (block + 1) * QROWS
        shape = (k1 - k0, QROWS)
        allowed = (doc_col_ref[k0:k1, :] == doc_row_ref[:, q0:q1]) & (
            iota2(shape, 0) + k0 <= iota2(shape, 1) + q0
        )
        bias[block, 0 : k1 - k0, :] = jnp.where(allowed, 0.0, NEG)


def attend_fwd_kernel(q_ref, k_ref, v_ref, doc_col_ref, doc_row_ref, out_ref, lse_ref, bias):
    blocks = q_ref.shape[0] // QROWS

    @pl.when(pl.program_id(0) == 0)
    def _():
        fill_bias(doc_col_ref, doc_row_ref, bias, blocks)

    for block in range(blocks):
        k0, k1 = key_span(block)
        q0, q1 = block * QROWS, (block + 1) * QROWS
        scores = mm_nt(k_ref[k0:k1, :], q_ref[q0:q1, :]) * HEAD_DIM ** (-0.5)
        scores = scores + bias[block, 0 : k1 - k0, :]
        top = jnp.max(scores, axis=0, keepdims=True)
        exponent = jnp.exp(scores - top)
        total = jnp.sum(exponent, axis=0, keepdims=True)
        probability = (exponent * (1.0 / total)).astype(bf16)
        out_ref[q0:q1, :] = mm_tn(v_ref[k0:k1, :], probability).T.astype(bf16)
        lse_ref[0, :, q0:q1] = top + jnp.log(total)


def attend_bwd_kernel(
    q_ref, k_ref, v_ref, do_ref, lse_ref, doc_col_ref, doc_row_ref, dq_ref, dk_ref, dv_ref, bias
):
    blocks = q_ref.shape[0] // QROWS

    @pl.when((pl.program_id(0) == 0) & (pl.program_id(1) == 0))
    def _():
        fill_bias(doc_col_ref, doc_row_ref, bias, blocks)

    @pl.when(pl.program_id(1) == 0)
    def _():
        dk_ref[...] = jnp.zeros_like(dk_ref)
        dv_ref[...] = jnp.zeros_like(dv_ref)

    for block in range(blocks):
        k0, k1 = key_span(block)
        q0, q1 = block * QROWS, (block + 1) * QROWS
        query = q_ref[q0:q1, :]
        key = k_ref[k0:k1, :]
        d_out = do_ref[q0:q1, :].astype(bf16)
        scores = mm_nt(key, query) * HEAD_DIM ** (-0.5) + bias[block, 0 : k1 - k0, :]
        probability = jnp.exp(scores - lse_ref[0, :, q0:q1])
        dv_ref[k0:k1, :] += mm(probability.astype(bf16), d_out)
        d_prob = mm_nt(v_ref[k0:k1, :], d_out)
        delta = jnp.sum(probability * d_prob, axis=0, keepdims=True)
        d_scores = (probability * (d_prob - delta) * HEAD_DIM ** (-0.5)).astype(bf16)
        dk_ref[k0:k1, :] += mm(d_scores, query)
        dq_ref[q0:q1, :] = mm_tn(key, d_scores).T


def attend_fwd(query, key, value, doc_col, doc_row):
    length = query.shape[0]
    group = HEADS // KV_HEADS
    blocks = length // QROWS
    return pl.pallas_call(
        attend_fwd_kernel,
        grid=(HEADS,),
        in_specs=[
            pl.BlockSpec((length, HEAD_DIM), lambda h: (0, h)),
            pl.BlockSpec((length, HEAD_DIM), lambda h: (0, h // group)),
            pl.BlockSpec((length, HEAD_DIM), lambda h: (0, h // group)),
            pl.BlockSpec((length, 1), lambda h: (0, 0)),
            pl.BlockSpec((1, length), lambda h: (0, 0)),
        ],
        out_specs=[
            pl.BlockSpec((length, HEAD_DIM), lambda h: (0, h)),
            pl.BlockSpec((1, 1, length), lambda h: (h, 0, 0)),
        ],
        out_shape=[
            jax.ShapeDtypeStruct((length, HEADS * HEAD_DIM), bf16),
            jax.ShapeDtypeStruct((HEADS, 1, length), f32),
        ],
        scratch_shapes=[pltpu.VMEM((blocks, QROWS + REACH, QROWS), f32)],
        compiler_params=pltpu.CompilerParams(vmem_limit_bytes=40 * 2**20),
    )(query, key, value, doc_col, doc_row)


def attend_bwd(query, key, value, d_out, lse, doc_col, doc_row):
    length = query.shape[0]
    group = HEADS // KV_HEADS
    blocks = length // QROWS
    per_query = pl.BlockSpec((length, HEAD_DIM), lambda g, r: (0, g * group + r))
    per_key = pl.BlockSpec((length, HEAD_DIM), lambda g, r: (0, g))
    return pl.pallas_call(
        attend_bwd_kernel,
        grid=(KV_HEADS, group),
        in_specs=[
            per_query,
            per_key,
            per_key,
            per_query,
            pl.BlockSpec((1, 1, length), lambda g, r: (g * group + r, 0, 0)),
            pl.BlockSpec((length, 1), lambda g, r: (0, 0)),
            pl.BlockSpec((1, length), lambda g, r: (0, 0)),
        ],
        out_specs=[per_query, per_key, per_key],
        out_shape=[
            jax.ShapeDtypeStruct((length, HEADS * HEAD_DIM), f32),
            jax.ShapeDtypeStruct((length, KV_HEADS * HEAD_DIM), f32),
            jax.ShapeDtypeStruct((length, KV_HEADS * HEAD_DIM), f32),
        ],
        scratch_shapes=[pltpu.VMEM((blocks, QROWS + REACH, QROWS), f32)],
        compiler_params=pltpu.CompilerParams(vmem_limit_bytes=40 * 2**20),
    )(query, key, value, d_out, lse, doc_col, doc_row)


def inv_norm(values):
    return lax.rsqrt(jnp.mean(values * values, axis=-1, keepdims=True) + eps)


def norm_back(normed_grad, gain, values, inv):
    unit = values * inv
    scaled = normed_grad * gain
    back = inv * (scaled - unit * jnp.mean(scaled * unit, axis=-1, keepdims=True))
    return back, jnp.sum(normed_grad * unit, axis=0)


def angles(length):
    half_dim = HEAD_DIM // 2
    frequency = rope_base ** (-jnp.arange(half_dim, dtype=f32) / half_dim)
    table = jnp.arange(length).astype(f32)[:, None] * frequency[None, :]
    return jnp.cos(table), jnp.sin(table)


def turn(values, cosine, sine):
    length, width = values.shape
    heads = values.reshape(length, width // HEAD_DIM, HEAD_DIM)
    front, back = jnp.split(heads, 2, axis=-1)
    cosine, sine = cosine[:, None, :], sine[:, None, :]
    turned = jnp.concatenate([front * cosine - back * sine, back * cosine + front * sine], axis=-1)
    return turned.reshape(length, width)


def silu_slope(values):
    gate = jax.nn.sigmoid(values)
    return gate * (1.0 + values * (1.0 - gate))


def same_doc(doc_ids, offset):
    earlier = jnp.pad(doc_ids, (offset, 0), constant_values=-1)[: doc_ids.shape[0]]
    return (earlier == doc_ids)[:, None]


def scatter(grads):
    return lax.psum_scatter(grads.astype(bf16), AXES, scatter_dimension=0, tiled=True).astype(f32)


def gather(parts):
    return lax.all_gather(jnp.concatenate(parts, axis=1), AXES, axis=0, tiled=True)


def shards(
    tokens, segments, cotangent, w_in, w_out, w_query, w_key, w_value, w_attn_out, w_gate, w_up,
    w_down, norm_in, conv_weight, conv_bias, dt_bias, a_log, skip_gain, norm_gated, norm_mid,
):
    length = tokens.shape[1]
    blocks = length // SPAN
    conv_end = D_SSM + CONV_CH
    rows_held = w_in.shape[0]
    dt_pad = jnp.zeros((rows_held, 128 - M_HEADS), bf16)
    w_first = gather(
        (w_in[:, :D_SSM], w_query, w_key, w_value, w_in[:, D_SSM:conv_end], w_in[:, conv_end:], dt_pad)
    )
    w_second = gather((w_attn_out.T, w_out.T))
    w_third = gather((w_gate, w_up))
    w_fourth = gather((w_down.T,))

    stream = tokens[0].astype(f32)
    doc_ids = segments[0]
    cot = cotangent[0]

    inv_in = inv_norm(stream)
    normed = (stream * inv_in * norm_in).astype(bf16)
    proj = mm(normed, w_first)
    z_gate = proj[:, :D_SSM]
    q_at, k_at, v_at = D_SSM, D_SSM + HEADS * HEAD_DIM, D_SSM + (HEADS + KV_HEADS) * HEAD_DIM
    conv_at = D_SSM + QKV
    dt_at = conv_at + CONV_CH
    conv_in = proj[:, conv_at:dt_at]
    cosine, sine = angles(length)
    query = turn(proj[:, q_at:k_at], cosine, sine).astype(bf16)
    key = turn(proj[:, k_at:v_at], cosine, sine).astype(bf16)
    value = proj[:, v_at:conv_at].astype(bf16)
    doc_float = doc_ids.astype(f32)
    doc_col, doc_row = doc_float[:, None], doc_float[None, :]
    attended, lse = attend_fwd(query, key, value, doc_col, doc_row)

    taps = conv_weight.shape[0]
    convolved = conv_bias[None, :] + conv_weight[0][None, :] * conv_in
    for offset in range(1, taps):
        shifted = jnp.pad(conv_in, ((offset, 0), (0, 0)))[:length]
        convolved = convolved + jnp.where(
            same_doc(doc_ids, offset), conv_weight[offset][None, :] * shifted, 0.0
        )
    act_low = jax.nn.silu(convolved).astype(bf16)
    x_heads = act_low[:, :D_SSM]
    raw = proj[:, dt_at : dt_at + M_HEADS] + dt_bias
    step_size = jax.nn.softplus(raw)
    log_decay = -step_size * jnp.exp(a_log)
    doc_blocks = doc_float.reshape(blocks, SPAN)
    last = doc_blocks[:, -1]
    prior = jnp.concatenate([jnp.full((1,), -1.0, f32), last[:-1]])
    wide_last = jnp.repeat(last, SPAN)[:, None]
    wide_prior = jnp.repeat(prior, SPAN)[:, None]
    ld = jnp.pad(log_decay, ((0, 0), (0, 128 - M_HEADS)))
    st = jnp.concatenate(
        [step_size, jnp.zeros((length, 125 - M_HEADS), f32), wide_last, wide_prior, doc_col], axis=1
    )
    scanned, states = scan_fwd(act_low, ld, st)
    skip_wide = jnp.repeat(skip_gain, M_HDIM)[None, :]
    ssm_out = scanned + skip_wide * x_heads.astype(f32)
    mixed_in = ssm_out * jax.nn.silu(z_gate)
    inv_gated = inv_norm(mixed_in)
    gated = (mixed_in * inv_gated * norm_gated).astype(bf16)
    branches = jnp.concatenate([attended, gated], axis=1)
    resid = stream + mm_nt(branches, w_second)
    inv_mid = inv_norm(resid)
    mid_in = (resid * inv_mid * norm_mid).astype(bf16)
    both = mm(mid_in, w_third)
    hidden_units = both.shape[1] // 2
    gate, up = both[:, :hidden_units], both[:, hidden_units:]
    hidden = (jax.nn.silu(gate) * up).astype(bf16)
    mixed = (resid + mm_nt(hidden, w_fourth)).astype(bf16)

    d_hidden = mm(cot, w_fourth)
    sum_fourth = scatter(mm_tn(cot, hidden))
    d_both = jnp.concatenate(
        [(d_hidden * up * silu_slope(gate)).astype(bf16), (d_hidden * jax.nn.silu(gate)).astype(bf16)],
        axis=1,
    )
    sum_third = scatter(mm_tn(mid_in, d_both))
    d_mid = mm_nt(d_both, w_third)
    back, g_norm_mid = norm_back(d_mid, norm_mid, resid, inv_mid)
    d_resid = cot.astype(f32) + back
    d_resid_low = d_resid.astype(bf16)
    sum_second = scatter(mm_tn(d_resid_low, branches))
    d_branches = mm(d_resid_low, w_second)
    attn_width = HEADS * HEAD_DIM
    d_query, d_key, d_value = attend_bwd(
        query, key, value, d_branches[:, :attn_width], lse, doc_col, doc_row
    )
    d_mixed_in, g_norm_gated = norm_back(d_branches[:, attn_width:], norm_gated, mixed_in, inv_gated)
    d_ssm = d_mixed_in * jax.nn.silu(z_gate)
    d_first = jnp.concatenate(
        [
            (d_mixed_in * ssm_out * silu_slope(z_gate)).astype(bf16),
            turn(d_query, cosine, -sine).astype(bf16),
            turn(d_key, cosine, -sine).astype(bf16),
            d_value.astype(bf16),
        ],
        axis=1,
    )
    sum_first = scatter(mm_tn(normed, d_first))
    g_skip = jnp.sum(jnp.sum(d_ssm * x_heads.astype(f32), axis=0).reshape(M_HEADS, M_HDIM), axis=1)
    d_x, d_b, d_c, d_st, d_ld = scan_bwd(act_low, ld, st, states, d_ssm)
    d_act = jnp.concatenate([d_x + skip_wide * d_ssm, d_b, d_c], axis=1)
    d_conv = d_act * silu_slope(convolved)
    g_conv_bias = jnp.sum(d_conv, axis=0)
    d_conv_in = conv_weight[0][None, :] * d_conv
    g_taps = [jnp.sum(d_conv * conv_in, axis=0)]
    for offset in range(1, taps):
        masked = jnp.where(same_doc(doc_ids, offset), d_conv, 0.0)
        shifted = jnp.pad(conv_in, ((offset, 0), (0, 0)))[:length]
        g_taps.append(jnp.sum(masked * shifted, axis=0))
        later = jnp.pad(masked, ((0, offset), (0, 0)))[offset:]
        d_conv_in = d_conv_in + conv_weight[offset][None, :] * later
    g_conv_weight = jnp.stack(g_taps)
    d_ld = d_ld[:, :M_HEADS]
    d_step = d_st[:, :M_HEADS] - d_ld * jnp.exp(a_log)
    g_a_log = jnp.sum(d_ld * log_decay, axis=0)
    d_raw = d_step * jax.nn.sigmoid(raw)
    g_dt_bias = jnp.sum(d_raw, axis=0)
    d_last = jnp.concatenate(
        [d_conv_in.astype(bf16), jnp.pad(d_raw, ((0, 0), (0, 128 - M_HEADS))).astype(bf16)], axis=1
    )
    sum_last = scatter(mm_tn(normed, d_last))
    d_normed = mm_nt(d_first, w_first[:, :conv_at]) + mm_nt(d_last, w_first[:, conv_at:])
    back, g_norm_in = norm_back(d_normed, norm_in, stream, inv_in)
    grad_tokens = d_resid + back

    small = (
        g_norm_in, g_conv_weight, g_conv_bias, g_dt_bias, g_a_log, g_skip, g_norm_gated, g_norm_mid
    )
    flat = jnp.concatenate([member.reshape(-1) for member in small])
    flat = lax.psum(jnp.pad(flat, (0, -flat.shape[0] % 1024)).reshape(-1, 128), AXES).reshape(-1)
    totals, at = [], 0
    for member in small:
        totals.append(flat[at : at + member.size].reshape(member.shape))
        at += member.size

    g_w_in = jnp.concatenate([sum_first[:, :D_SSM], sum_last[:, : CONV_CH + M_HEADS]], axis=1)
    return (
        mixed[None],
        grad_tokens[None],
        g_w_in,
        sum_second[:, attn_width:].T,
        sum_first[:, q_at:k_at],
        sum_first[:, k_at:v_at],
        sum_first[:, v_at:],
        sum_second[:, :attn_width].T,
        sum_third[:, :hidden_units],
        sum_third[:, hidden_units:],
        sum_fourth.T,
    ) + tuple(totals)


def solution(mesh):
    rows = P(AXES, None)
    cols = P(None, AXES)
    whole = P(AXES, None, None)
    weights = (rows, cols, rows, rows, rows, cols, rows, rows, cols)
    in_specs = (whole, rows, whole) + weights + (P(),) * 8
    out_specs = (whole, whole) + weights + (P(),) * 8
    return jax.shard_map(shards, mesh=mesh, in_specs=in_specs, out_specs=out_specs, check_vma=False)
```

```python
from functools import partial

import jax
import jax.numpy as jnp
from jax import lax
from jax.experimental import pallas as pl
from jax.experimental.pallas import tpu as pltpu
from jax.sharding import PartitionSpec as P

HEADS = 8
KV_HEADS = 2
HEAD_DIM = 128
M_HEADS = 24
M_HDIM = 64
STATE = 128
SPAN = 128
D_SSM = 1536
CONV_CH = 1792
QKV = (HEADS + 2 * KV_HEADS) * HEAD_DIM
PAIRS = M_HEADS // 2
QROWS = 256
REACH = 512

AXES = ("fsdp", "dp")
bf16 = jnp.bfloat16
f32 = jnp.float32
eps = 1e-06
rope_base = 100000000000.0
NEG = -1e30

NT = (((1,), (1,)), ((), ()))
TN = (((0,), (0,)), ((), ()))


def mm(left, right):
    return jnp.dot(left, right, preferred_element_type=f32)


def mm_nt(left, right):
    return lax.dot_general(left, right, NT, preferred_element_type=f32)


def mm_tn(left, right):
    return lax.dot_general(left, right, TN, preferred_element_type=f32)


def exact_mm(left, right):
    return jnp.dot(left, right, precision=lax.Precision.HIGHEST, preferred_element_type=f32)


def split_mm(value, selector):
    high = value.astype(bf16)
    low = (value - high.astype(f32)).astype(bf16)
    return mm(high, selector) + mm(low, selector)


def iota2(shape, axis):
    return lax.broadcasted_iota(jnp.int32, shape, axis)


def head_spread():
    rows = iota2((SPAN, D_SSM), 0)
    cols = iota2((SPAN, D_SSM), 1)
    return jnp.where(cols // M_HDIM == rows, 1.0, 0.0).astype(bf16)


def head_gather():
    rows = iota2((D_SSM, SPAN), 0)
    cols = iota2((D_SSM, SPAN), 1)
    return jnp.where(rows // M_HDIM == cols, 1.0, 0.0).astype(bf16)


def split_pair(block):
    lanes = iota2(block.shape, 1)
    zero = jnp.zeros_like(block)
    return jnp.concatenate(
        [jnp.where(lanes < M_HDIM, block, zero), jnp.where(lanes < M_HDIM, zero, block)], axis=0
    )


def block_terms(ld_ref, st_ref, spread):
    ld = ld_ref[...]
    st = st_ref[...]
    rows = iota2((SPAN, SPAN), 0)
    cols = iota2((SPAN, SPAN), 1)
    cum = exact_mm(jnp.where(rows >= cols, 1.0, 0.0), ld)
    cum_t = cum.T
    st_t = st.T
    doc = st[:, 127:128]
    prior = st[:, 126:127]
    last = st[:, 125:126]
    doc_row = st_t[127:128, :]
    carried = jnp.where(doc == prior, jnp.exp(cum), 0.0)
    gap = jnp.where(doc == last, jnp.exp(cum[SPAN - 1 : SPAN, :] - cum), 0.0)
    keep = jnp.where(last == prior, jnp.exp(cum[SPAN - 1 : SPAN, :]), 0.0)
    keep = keep[0:8, :]
    return (st, cum, cum_t, st_t, doc, doc_row, carried, gap, keep)


def scan_fwd_kernel(x_ref, b_ref, c_ref, ld_ref, st_ref, y_ref, states_ref, state):
    spread = head_spread()

    @pl.when(pl.program_id(0) == 0)
    def _():
        state[...] = jnp.zeros_like(state)

    st, cum, cum_t, st_t, doc, doc_row, carried, gap, keep = block_terms(ld_ref, st_ref, spread)
    rows = iota2((SPAN, SPAN), 0)
    cols = iota2((SPAN, SPAN), 1)
    bias = jnp.where((doc == doc_row) & (rows >= cols), 0.0, NEG)
    b_blk = b_ref[...]
    c_blk = c_ref[...]
    affinity = mm_nt(c_blk, b_blk)
    old = state[...]
    old_low = old.astype(bf16)
    states_ref[0] = old_low
    from_state = mm(c_blk, old_low) * split_mm(carried, spread)
    for pair in range(PAIRS):
        lo, hi = pair * SPAN, (pair + 1) * SPAN
        mats = []
        for h in (2 * pair, 2 * pair + 1):
            decay = jnp.exp(cum[:, h : h + 1] - cum_t[h : h + 1, :] + bias)
            mats.append((affinity * decay * st_t[h : h + 1, :]).astype(bf16))
        inside = mm(jnp.concatenate(mats, axis=1), split_pair(x_ref[:, lo:hi]))
        y_ref[:, lo:hi] = inside + from_state[:, lo:hi]
    tail = split_mm(gap * st, spread)
    pushed = (x_ref[...].astype(f32) * tail).astype(bf16)
    state[...] = old * split_mm(keep, spread)[0:1, :] + mm_tn(b_blk, pushed)


def scan_bwd_kernel(
    x_ref, b_ref, c_ref, ld_ref, st_ref, states_ref, dy_ref,
    dx_ref, db_ref, dc_ref, dst_ref, dld_ref, dstate, grow, gcol,
):
    spread = head_spread()
    gather = head_gather()

    @pl.when(pl.program_id(0) == 0)
    def _():
        dstate[...] = jnp.zeros_like(dstate)
        grow[...] = jnp.zeros_like(grow)
        gcol[...] = jnp.zeros_like(gcol)

    st, cum, cum_t, st_t, doc, doc_row, carried, gap, keep = block_terms(ld_ref, st_ref, spread)
    rows = iota2((SPAN, SPAN), 0)
    cols = iota2((SPAN, SPAN), 1)
    bias = jnp.where((doc == doc_row) & (cols >= rows), 0.0, NEG)
    b_blk = b_ref[...]
    c_blk = c_ref[...]
    x_blk = x_ref[...]
    dy = dy_ref[...]
    dy_low = dy.astype(bf16)
    affinity = mm_nt(b_blk, c_blk)
    old_low = states_ref[0]
    d_new = dstate[...]
    d_new_low = d_new.astype(bf16)
    carried_wide = split_mm(carried, spread)
    tail_wide = split_mm(gap * st, spread)
    keep_wide = split_mm(keep, spread)[0:1, :]
    from_tail = mm(b_blk, d_new_low)
    d_aff = jnp.zeros((SPAN, SPAN), f32)
    for pair in range(PAIRS):
        lo, hi = pair * SPAN, (pair + 1) * SPAN
        d_mats = mm_nt(split_pair(x_blk[:, lo:hi]), dy_low[:, lo:hi])
        mats = []
        for which, h in enumerate((2 * pair, 2 * pair + 1)):
            step = st[:, h : h + 1]
            decay = jnp.exp(cum_t[h : h + 1, :] - cum[:, h : h + 1] + bias)
            scaled = affinity * decay
            mats.append((scaled * step).astype(bf16))
            d_mat = d_mats[which * SPAN : (which + 1) * SPAN, :]
            d_aff = d_aff + d_mat * decay * step
            products = d_mat * scaled
            gcol[:, h : h + 1] = jnp.sum(products, axis=1, keepdims=True)
            grow[h : h + 1, :] = jnp.sum(products * step, axis=0, keepdims=True)
        inside = mm(jnp.concatenate(mats, axis=1), split_pair(dy_low[:, lo:hi]))
        dx_ref[:, lo:hi] = inside + from_tail[:, lo:hi] * tail_wide[:, lo:hi]
    flowing = dy * carried_wide
    flowing_low = flowing.astype(bf16)
    d_cum = split_mm(flowing * mm(c_blk, old_low), gather)
    d_tail = split_mm(x_blk.astype(f32) * from_tail, gather)
    moved = d_tail * gap * st
    d_keep = jnp.sum(d_new * old_low.astype(f32), axis=0, keepdims=True)
    d_keep = split_mm(jnp.broadcast_to(d_keep, (8, D_SSM)), gather) * keep
    at_end = jnp.sum(moved, axis=0, keepdims=True) + d_keep[0:1, :]
    d_cum = d_cum - moved + grow[...].T - gcol[...] * st
    d_cum = d_cum + jnp.where(rows == SPAN - 1, at_end, 0.0)
    dst_ref[...] = gcol[...] + d_tail * gap
    dld_ref[...] = exact_mm(jnp.where(cols >= rows, 1.0, 0.0), d_cum)
    d_aff_low = d_aff.astype(bf16)
    pushed = (x_blk.astype(f32) * tail_wide).astype(bf16)
    dc_ref[...] = mm_tn(d_aff_low, b_blk) + mm_nt(flowing_low, old_low)
    db_ref[...] = mm(d_aff_low, c_blk) + mm_nt(pushed, d_new_low)
    dstate[...] = d_new * keep_wide + mm_tn(c_blk, flowing_low)


def scan_fwd(act_low, ld, st):
    length = act_low.shape[0]
    blocks = length // SPAN
    return pl.pallas_call(
        scan_fwd_kernel,
        grid=(blocks,),
        in_specs=[
            pl.BlockSpec((SPAN, D_SSM), lambda i: (i, 0)),
            pl.BlockSpec((SPAN, STATE), lambda i: (i, D_SSM // STATE)),
            pl.BlockSpec((SPAN, STATE), lambda i: (i, D_SSM // STATE + 1)),
            pl.BlockSpec((SPAN, 128), lambda i: (i, 0)),
            pl.BlockSpec((SPAN, 128), lambda i: (i, 0)),
        ],
        out_specs=[
            pl.BlockSpec((SPAN, D_SSM), lambda i: (i, 0)),
            pl.BlockSpec((1, STATE, D_SSM), lambda i: (i, 0, 0)),
        ],
        out_shape=[
            jax.ShapeDtypeStruct((length, D_SSM), f32),
            jax.ShapeDtypeStruct((blocks, STATE, D_SSM), bf16),
        ],
        scratch_shapes=[pltpu.VMEM((STATE, D_SSM), f32)],
        compiler_params=pltpu.CompilerParams(vmem_limit_bytes=40 * 2**20),
    )(act_low, act_low, act_low, ld, st)


def scan_bwd(act_low, ld, st, states, dy):
    length = act_low.shape[0]
    blocks = length // SPAN
    end = blocks - 1
    return pl.pallas_call(
        scan_bwd_kernel,
        grid=(blocks,),
        in_specs=[
            pl.BlockSpec((SPAN, D_SSM), lambda i: (end - i, 0)),
            pl.BlockSpec((SPAN, STATE), lambda i: (end - i, D_SSM // STATE)),
            pl.BlockSpec((SPAN, STATE), lambda i: (end - i, D_SSM // STATE + 1)),
            pl.BlockSpec((SPAN, 128), lambda i: (end - i, 0)),
            pl.BlockSpec((SPAN, 128), lambda i: (end - i, 0)),
            pl.BlockSpec((1, STATE, D_SSM), lambda i: (end - i, 0, 0)),
            pl.BlockSpec((SPAN, D_SSM), lambda i: (end - i, 0)),
        ],
        out_specs=[
            pl.BlockSpec((SPAN, D_SSM), lambda i: (end - i, 0)),
            pl.BlockSpec((SPAN, STATE), lambda i: (end - i, 0)),
            pl.BlockSpec((SPAN, STATE), lambda i: (end - i, 0)),
            pl.BlockSpec((SPAN, 128), lambda i: (end - i, 0)),
            pl.BlockSpec((SPAN, 128), lambda i: (end - i, 0)),
        ],
        out_shape=[
            jax.ShapeDtypeStruct((length, D_SSM), f32),
            jax.ShapeDtypeStruct((length, STATE), f32),
            jax.ShapeDtypeStruct((length, STATE), f32),
            jax.ShapeDtypeStruct((length, 128), f32),
            jax.ShapeDtypeStruct((length, 128), f32),
        ],
        scratch_shapes=[
            pltpu.VMEM((STATE, D_SSM), f32),
            pltpu.VMEM((SPAN, SPAN), f32),
            pltpu.VMEM((SPAN, SPAN), f32),
        ],
        compiler_params=pltpu.CompilerParams(vmem_limit_bytes=40 * 2**20),
    )(act_low, act_low, act_low, ld, st, states, dy)


def key_span(block):
    return max(0, block * QROWS - REACH), (block + 1) * QROWS


def fill_bias(doc_col_ref, doc_row_ref, bias, blocks):
    for block in range(blocks):
        k0, k1 = key_span(block)
        q0, q1 = block * QROWS, (block + 1) * QROWS
        shape = (k1 - k0, QROWS)
        allowed = (doc_col_ref[k0:k1, :] == doc_row_ref[:, q0:q1]) & (
            iota2(shape, 0) + k0 <= iota2(shape, 1) + q0
        )
        bias[block, 0 : k1 - k0, :] = jnp.where(allowed, 0.0, NEG)


def attend_fwd_kernel(q_ref, k_ref, v_ref, doc_col_ref, doc_row_ref, out_ref, lse_ref, bias):
    blocks = q_ref.shape[0] // QROWS

    @pl.when(pl.program_id(0) == 0)
    def _():
        fill_bias(doc_col_ref, doc_row_ref, bias, blocks)

    for block in range(blocks):
        k0, k1 = key_span(block)
        q0, q1 = block * QROWS, (block + 1) * QROWS
        scores = mm_nt(k_ref[k0:k1, :], q_ref[q0:q1, :]) * HEAD_DIM ** (-0.5)
        scores = scores + bias[block, 0 : k1 - k0, :]
        top = jnp.max(scores, axis=0, keepdims=True)
        exponent = jnp.exp(scores - top)
        total = jnp.sum(exponent, axis=0, keepdims=True)
        probability = (exponent * (1.0 / total)).astype(bf16)
        out_ref[q0:q1, :] = mm_tn(v_ref[k0:k1, :], probability).T.astype(bf16)
        lse_ref[0, :, q0:q1] = top + jnp.log(total)


def attend_bwd_kernel(
    q_ref, k_ref, v_ref, do_ref, lse_ref, doc_col_ref, doc_row_ref, dq_ref, dk_ref, dv_ref, bias
):
    blocks = q_ref.shape[0] // QROWS

    @pl.when((pl.program_id(0) == 0) & (pl.program_id(1) == 0))
    def _():
        fill_bias(doc_col_ref, doc_row_ref, bias, blocks)

    @pl.when(pl.program_id(1) == 0)
    def _():
        dk_ref[...] = jnp.zeros_like(dk_ref)
        dv_ref[...] = jnp.zeros_like(dv_ref)

    for block in range(blocks):
        k0, k1 = key_span(block)
        q0, q1 = block * QROWS, (block + 1) * QROWS
        query = q_ref[q0:q1, :]
        key = k_ref[k0:k1, :]
        d_out = do_ref[q0:q1, :].astype(bf16)
        scores = mm_nt(key, query) * HEAD_DIM ** (-0.5) + bias[block, 0 : k1 - k0, :]
        probability = jnp.exp(scores - lse_ref[0, :, q0:q1])
        dv_ref[k0:k1, :] += mm(probability.astype(bf16), d_out)
        d_prob = mm_nt(v_ref[k0:k1, :], d_out)
        delta = jnp.sum(probability * d_prob, axis=0, keepdims=True)
        d_scores = (probability * (d_prob - delta) * HEAD_DIM ** (-0.5)).astype(bf16)
        dk_ref[k0:k1, :] += mm(d_scores, query)
        dq_ref[q0:q1, :] = mm_tn(key, d_scores).T


def attend_fwd(query, key, value, doc_col, doc_row):
    length = query.shape[0]
    group = HEADS // KV_HEADS
    blocks = length // QROWS
    return pl.pallas_call(
        attend_fwd_kernel,
        grid=(HEADS,),
        in_specs=[
            pl.BlockSpec((length, HEAD_DIM), lambda h: (0, h)),
            pl.BlockSpec((length, HEAD_DIM), lambda h: (0, h // group)),
            pl.BlockSpec((length, HEAD_DIM), lambda h: (0, h // group)),
            pl.BlockSpec((length, 1), lambda h: (0, 0)),
            pl.BlockSpec((1, length), lambda h: (0, 0)),
        ],
        out_specs=[
            pl.BlockSpec((length, HEAD_DIM), lambda h: (0, h)),
            pl.BlockSpec((1, 1, length), lambda h: (h, 0, 0)),
        ],
        out_shape=[
            jax.ShapeDtypeStruct((length, HEADS * HEAD_DIM), bf16),
            jax.ShapeDtypeStruct((HEADS, 1, length), f32),
        ],
        scratch_shapes=[pltpu.VMEM((blocks, QROWS + REACH, QROWS), f32)],
        compiler_params=pltpu.CompilerParams(vmem_limit_bytes=40 * 2**20),
    )(query, key, value, doc_col, doc_row)


def attend_bwd(query, key, value, d_out, lse, doc_col, doc_row):
    length = query.shape[0]
    group = HEADS // KV_HEADS
    blocks = length // QROWS
    per_query = pl.BlockSpec((length, HEAD_DIM), lambda g, r: (0, g * group + r))
    per_key = pl.BlockSpec((length, HEAD_DIM), lambda g, r: (0, g))
    return pl.pallas_call(
        attend_bwd_kernel,
        grid=(KV_HEADS, group),
        in_specs=[
            per_query,
            per_key,
            per_key,
            per_query,
            pl.BlockSpec((1, 1, length), lambda g, r: (g * group + r, 0, 0)),
            pl.BlockSpec((length, 1), lambda g, r: (0, 0)),
            pl.BlockSpec((1, length), lambda g, r: (0, 0)),
        ],
        out_specs=[per_query, per_key, per_key],
        out_shape=[
            jax.ShapeDtypeStruct((length, HEADS * HEAD_DIM), f32),
            jax.ShapeDtypeStruct((length, KV_HEADS * HEAD_DIM), f32),
            jax.ShapeDtypeStruct((length, KV_HEADS * HEAD_DIM), f32),
        ],
        scratch_shapes=[pltpu.VMEM((blocks, QROWS + REACH, QROWS), f32)],
        compiler_params=pltpu.CompilerParams(vmem_limit_bytes=40 * 2**20),
    )(query, key, value, d_out, lse, doc_col, doc_row)


def inv_norm(values):
    return lax.rsqrt(jnp.mean(values * values, axis=-1, keepdims=True) + eps)


def norm_back(normed_grad, gain, values, inv):
    unit = values * inv
    scaled = normed_grad * gain
    back = inv * (scaled - unit * jnp.mean(scaled * unit, axis=-1, keepdims=True))
    return back, jnp.sum(normed_grad * unit, axis=0)


def angles(length):
    half_dim = HEAD_DIM // 2
    frequency = rope_base ** (-jnp.arange(half_dim, dtype=f32) / half_dim)
    table = jnp.arange(length).astype(f32)[:, None] * frequency[None, :]
    return jnp.cos(table), jnp.sin(table)


def turn(values, cosine, sine):
    length, width = values.shape
    heads = values.reshape(length, width // HEAD_DIM, HEAD_DIM)
    front, back = jnp.split(heads, 2, axis=-1)
    cosine, sine = cosine[:, None, :], sine[:, None, :]
    turned = jnp.concatenate([front * cosine - back * sine, back * cosine + front * sine], axis=-1)
    return turned.reshape(length, width)


def silu_slope(values):
    gate = jax.nn.sigmoid(values)
    return gate * (1.0 + values * (1.0 - gate))


def same_doc(doc_ids, offset):
    earlier = jnp.pad(doc_ids, (offset, 0), constant_values=-1)[: doc_ids.shape[0]]
    return (earlier == doc_ids)[:, None]


def flip(values, bit):
    places = lax.axis_size(AXES)
    return lax.ppermute(values, AXES, [(i, i ^ bit) for i in range(places)])


def add(left, right):
    return (left.astype(f32) + right.astype(f32)).astype(bf16)


def at(values, index, axis):
    return lax.dynamic_index_in_dim(values, index, axis, keepdims=False)


def scatter(grads):
    dp = lax.axis_size("dp")
    chips = lax.axis_size("fsdp") // 2
    if dp != 2 or chips < 4:
        return lax.psum_scatter(grads, AXES, scatter_dimension=0, tiled=True).astype(f32)
    rows, width = grads.shape
    held = rows // (4 * chips)
    place = lax.axis_index("fsdp")
    core, y, z, x = place % 2, (place // 2) % 2, place // 4, lax.axis_index("dp")
    blocks = grads.reshape(chips, 2, 2 * held, width)
    shape = (chips // 2, 2, 2, held, width)
    own = at(blocks, core, 1).reshape(shape)
    other = flip(at(blocks, 1 - core, 1), 2).reshape(shape)

    def pick(row, col):
        zero = jnp.zeros((), place.dtype)
        start, size = (zero, row, col, zero, zero), (chips // 2, 1, 1, held, width)
        return add(lax.dynamic_slice(own, start, size), lax.dynamic_slice(other, start, size))[:, 0, 0]

    def along(first):
        return jnp.stack(
            [
                pick(jnp.where(core == 0, second, first), jnp.where(core == 0, first, second))
                for second in jnp.arange(2, dtype=place.dtype)
            ]
        )

    near = jnp.where(core == 0, x, y)
    far = jnp.where(core == 0, y, x)
    places = 4 * chips
    crossing = [(i, i ^ (4 if i & 2 else 1)) for i in range(places)]
    back = [(i, i ^ (1 if i & 2 else 4)) for i in range(places)]
    sent, own = along(1 - near), along(near)
    other = lax.ppermute(sent, AXES, crossing)
    sent = add(at(own, 1 - far, 0), at(other, 1 - far, 0))
    own = add(at(own, far, 0), at(other, far, 0))
    other = lax.ppermute(sent, AXES, back)
    level = 1
    while level < chips // 2:
        shape = (-1, 2, held, width)
        mine = (z // level) % 2
        own, other = own.reshape(shape), other.reshape(shape)
        sent = add(at(own, 1 - mine, 1), at(other, 1 - mine, 1))
        own = add(at(own, mine, 1), at(other, mine, 1))
        other = flip(sent, 8 * level)
        level *= 2
    return (own.astype(f32) + other.astype(f32)).reshape(held, width)


def sum_everywhere(values):
    bit = 1
    while bit < lax.axis_size(AXES):
        values = values + flip(values, bit)
        bit *= 2
    return values


def gather(parts):
    return lax.all_gather(jnp.concatenate(parts, axis=1), AXES, axis=0, tiled=True)


def shards(
    tokens, segments, cotangent, w_in, w_out, w_query, w_key, w_value, w_attn_out, w_gate, w_up,
    w_down, norm_in, conv_weight, conv_bias, dt_bias, a_log, skip_gain, norm_gated, norm_mid,
):
    length = tokens.shape[1]
    blocks = length // SPAN
    conv_end = D_SSM + CONV_CH
    rows_held = w_in.shape[0]
    dt_pad = jnp.zeros((rows_held, 128 - M_HEADS), bf16)
    w_first = gather(
        (w_in[:, :D_SSM], w_query, w_key, w_value, w_in[:, D_SSM:conv_end], w_in[:, conv_end:], dt_pad)
    )
    w_second = gather((w_attn_out.T, w_out.T))
    w_third = gather((w_gate, w_up))
    w_fourth = gather((w_down.T,))

    stream = tokens[0].astype(f32)
    doc_ids = segments[0]
    cot = cotangent[0]

    inv_in = inv_norm(stream)
    normed = (stream * inv_in * norm_in).astype(bf16)
    proj = mm(normed, w_first)
    z_gate = proj[:, :D_SSM]
    q_at, k_at, v_at = D_SSM, D_SSM + HEADS * HEAD_DIM, D_SSM + (HEADS + KV_HEADS) * HEAD_DIM
    conv_at = D_SSM + QKV
    dt_at = conv_at + CONV_CH
    conv_in = proj[:, conv_at:dt_at]
    cosine, sine = angles(length)
    query = turn(proj[:, q_at:k_at], cosine, sine).astype(bf16)
    key = turn(proj[:, k_at:v_at], cosine, sine).astype(bf16)
    value = proj[:, v_at:conv_at].astype(bf16)
    doc_float = doc_ids.astype(f32)
    doc_col, doc_row = doc_float[:, None], doc_float[None, :]
    attended, lse = attend_fwd(query, key, value, doc_col, doc_row)

    taps = conv_weight.shape[0]
    convolved = conv_bias[None, :] + conv_weight[0][None, :] * conv_in
    for offset in range(1, taps):
        shifted = jnp.pad(conv_in, ((offset, 0), (0, 0)))[:length]
        convolved = convolved + jnp.where(
            same_doc(doc_ids, offset), conv_weight[offset][None, :] * shifted, 0.0
        )
    act_low = jax.nn.silu(convolved).astype(bf16)
    x_heads = act_low[:, :D_SSM]
    raw = proj[:, dt_at : dt_at + M_HEADS] + dt_bias
    step_size = jax.nn.softplus(raw)
    log_decay = -step_size * jnp.exp(a_log)
    doc_blocks = doc_float.reshape(blocks, SPAN)
    last = doc_blocks[:, -1]
    prior = jnp.concatenate([jnp.full((1,), -1.0, f32), last[:-1]])
    wide_last = jnp.repeat(last, SPAN)[:, None]
    wide_prior = jnp.repeat(prior, SPAN)[:, None]
    ld = jnp.pad(log_decay, ((0, 0), (0, 128 - M_HEADS)))
    st = jnp.concatenate(
        [step_size, jnp.zeros((length, 125 - M_HEADS), f32), wide_last, wide_prior, doc_col], axis=1
    )
    scanned, states = scan_fwd(act_low, ld, st)
    skip_wide = jnp.repeat(skip_gain, M_HDIM)[None, :]
    ssm_out = scanned + skip_wide * x_heads.astype(f32)
    mixed_in = ssm_out * jax.nn.silu(z_gate)
    inv_gated = inv_norm(mixed_in)
    gated = (mixed_in * inv_gated * norm_gated).astype(bf16)
    branches = jnp.concatenate([attended, gated], axis=1)
    resid = stream + mm_nt(branches, w_second)
    inv_mid = inv_norm(resid)
    mid_in = (resid * inv_mid * norm_mid).astype(bf16)
    both = mm(mid_in, w_third)
    hidden_units = both.shape[1] // 2
    gate, up = both[:, :hidden_units], both[:, hidden_units:]
    hidden = (jax.nn.silu(gate) * up).astype(bf16)
    mixed = (resid + mm_nt(hidden, w_fourth)).astype(bf16)

    d_hidden = mm(cot, w_fourth)
    sum_fourth = scatter(mm_tn(cot, hidden).astype(bf16))
    d_both = jnp.concatenate(
        [(d_hidden * up * silu_slope(gate)).astype(bf16), (d_hidden * jax.nn.silu(gate)).astype(bf16)],
        axis=1,
    )
    sum_third = scatter(mm_tn(mid_in, d_both).astype(bf16))
    d_mid = mm_nt(d_both, w_third)
    back, g_norm_mid = norm_back(d_mid, norm_mid, resid, inv_mid)
    d_resid = cot.astype(f32) + back
    d_resid_low = d_resid.astype(bf16)
    sum_second = scatter(mm_tn(d_resid_low, branches).astype(bf16))
    d_branches = mm(d_resid_low, w_second)
    attn_width = HEADS * HEAD_DIM
    d_query, d_key, d_value = attend_bwd(
        query, key, value, d_branches[:, :attn_width], lse, doc_col, doc_row
    )
    d_mixed_in, g_norm_gated = norm_back(d_branches[:, attn_width:], norm_gated, mixed_in, inv_gated)
    d_ssm = d_mixed_in * jax.nn.silu(z_gate)
    d_first = jnp.concatenate(
        [
            (d_mixed_in * ssm_out * silu_slope(z_gate)).astype(bf16),
            turn(d_query, cosine, -sine).astype(bf16),
            turn(d_key, cosine, -sine).astype(bf16),
            d_value.astype(bf16),
        ],
        axis=1,
    )
    sum_first = scatter(mm_tn(normed, d_first).astype(bf16))
    g_skip = jnp.sum(jnp.sum(d_ssm * x_heads.astype(f32), axis=0).reshape(M_HEADS, M_HDIM), axis=1)
    d_x, d_b, d_c, d_st, d_ld = scan_bwd(act_low, ld, st, states, d_ssm)
    d_act = jnp.concatenate([d_x + skip_wide * d_ssm, d_b, d_c], axis=1)
    d_conv = d_act * silu_slope(convolved)
    g_conv_bias = jnp.sum(d_conv, axis=0)
    d_conv_in = conv_weight[0][None, :] * d_conv
    g_taps = [jnp.sum(d_conv * conv_in, axis=0)]
    for offset in range(1, taps):
        masked = jnp.where(same_doc(doc_ids, offset), d_conv, 0.0)
        shifted = jnp.pad(conv_in, ((offset, 0), (0, 0)))[:length]
        g_taps.append(jnp.sum(masked * shifted, axis=0))
        later = jnp.pad(masked, ((0, offset), (0, 0)))[offset:]
        d_conv_in = d_conv_in + conv_weight[offset][None, :] * later
    g_conv_weight = jnp.stack(g_taps)
    d_ld = d_ld[:, :M_HEADS]
    d_step = d_st[:, :M_HEADS] - d_ld * jnp.exp(a_log)
    g_a_log = jnp.sum(d_ld * log_decay, axis=0)
    d_raw = d_step * jax.nn.sigmoid(raw)
    g_dt_bias = jnp.sum(d_raw, axis=0)
    d_last = jnp.concatenate(
        [d_conv_in.astype(bf16), jnp.pad(d_raw, ((0, 0), (0, 128 - M_HEADS))).astype(bf16)], axis=1
    )
    sum_last = scatter(mm_tn(normed, d_last).astype(bf16))
    d_normed = mm_nt(d_first, w_first[:, :conv_at]) + mm_nt(d_last, w_first[:, conv_at:])
    back, g_norm_in = norm_back(d_normed, norm_in, stream, inv_in)
    grad_tokens = d_resid + back

    small = (
        g_norm_in, g_conv_weight, g_conv_bias, g_dt_bias, g_a_log, g_skip, g_norm_gated, g_norm_mid
    )
    flat = jnp.concatenate([member.reshape(-1) for member in small])
    flat = sum_everywhere(jnp.pad(flat, (0, -flat.shape[0] % 1024)).reshape(-1, 128)).reshape(-1)
    totals, at = [], 0
    for member in small:
        totals.append(flat[at : at + member.size].reshape(member.shape))
        at += member.size

    g_w_in = jnp.concatenate([sum_first[:, :D_SSM], sum_last[:, : CONV_CH + M_HEADS]], axis=1)
    return (
        mixed[None],
        grad_tokens[None],
        g_w_in,
        sum_second[:, attn_width:].T,
        sum_first[:, q_at:k_at],
        sum_first[:, k_at:v_at],
        sum_first[:, v_at:],
        sum_second[:, :attn_width].T,
        sum_third[:, :hidden_units],
        sum_third[:, hidden_units:],
        sum_fourth.T,
    ) + tuple(totals)


def solution(mesh):
    rows = P(AXES, None)
    cols = P(None, AXES)
    whole = P(AXES, None, None)
    weights = (rows, cols, rows, rows, rows, cols, rows, rows, cols)
    in_specs = (whole, rows, whole) + weights + (P(),) * 8
    out_specs = (whole, whole) + weights + (P(),) * 8
    return jax.shard_map(shards, mesh=mesh, in_specs=in_specs, out_specs=out_specs, check_vma=False)
```

```python
from functools import partial

import jax
import jax.numpy as jnp
from jax import lax
from jax.experimental import pallas as pl
from jax.experimental.pallas import tpu as pltpu
from jax.sharding import PartitionSpec as P

HEADS = 8
KV_HEADS = 2
HEAD_DIM = 128
M_HEADS = 24
M_HDIM = 64
STATE = 128
SPAN = 128
D_SSM = 1536
CONV_CH = 1792
QKV = (HEADS + 2 * KV_HEADS) * HEAD_DIM
PAIRS = M_HEADS // 2
QROWS = 256
REACH = 512

AXES = ("fsdp", "dp")
bf16 = jnp.bfloat16
f32 = jnp.float32
eps = 1e-06
rope_base = 100000000000.0
NEG = -1e30

NT = (((1,), (1,)), ((), ()))
TN = (((0,), (0,)), ((), ()))


def mm(left, right):
    return jnp.dot(left, right, preferred_element_type=f32)


def mm_nt(left, right):
    return lax.dot_general(left, right, NT, preferred_element_type=f32)


def mm_tn(left, right):
    return lax.dot_general(left, right, TN, preferred_element_type=f32)


def exact_mm(left, right):
    return jnp.dot(left, right, precision=lax.Precision.HIGHEST, preferred_element_type=f32)


def split_mm(value, selector):
    high = value.astype(bf16)
    low = (value - high.astype(f32)).astype(bf16)
    return mm(high, selector) + mm(low, selector)


def iota2(shape, axis):
    return lax.broadcasted_iota(jnp.int32, shape, axis)


def head_spread():
    rows = iota2((SPAN, D_SSM), 0)
    cols = iota2((SPAN, D_SSM), 1)
    return jnp.where(cols // M_HDIM == rows, 1.0, 0.0).astype(bf16)


def head_gather():
    rows = iota2((D_SSM, SPAN), 0)
    cols = iota2((D_SSM, SPAN), 1)
    return jnp.where(rows // M_HDIM == cols, 1.0, 0.0).astype(bf16)


def split_pair(block):
    lanes = iota2(block.shape, 1)
    zero = jnp.zeros_like(block)
    return jnp.concatenate(
        [jnp.where(lanes < M_HDIM, block, zero), jnp.where(lanes < M_HDIM, zero, block)], axis=0
    )


def block_terms(ld_ref, st_ref, spread):
    ld = ld_ref[...]
    st = st_ref[...]
    rows = iota2((SPAN, SPAN), 0)
    cols = iota2((SPAN, SPAN), 1)
    cum = exact_mm(jnp.where(rows >= cols, 1.0, 0.0), ld)
    cum_t = cum.T
    st_t = st.T
    doc = st[:, 127:128]
    prior = st[:, 126:127]
    last = st[:, 125:126]
    doc_row = st_t[127:128, :]
    carried = jnp.where(doc == prior, jnp.exp(cum), 0.0)
    gap = jnp.where(doc == last, jnp.exp(cum[SPAN - 1 : SPAN, :] - cum), 0.0)
    keep = jnp.where(last == prior, jnp.exp(cum[SPAN - 1 : SPAN, :]), 0.0)
    keep = keep[0:8, :]
    return (st, cum, cum_t, st_t, doc, doc_row, carried, gap, keep)


def scan_fwd_kernel(x_ref, b_ref, c_ref, ld_ref, st_ref, y_ref, states_ref, state):
    spread = head_spread()

    @pl.when(pl.program_id(0) == 0)
    def _():
        state[...] = jnp.zeros_like(state)

    st, cum, cum_t, st_t, doc, doc_row, carried, gap, keep = block_terms(ld_ref, st_ref, spread)
    rows = iota2((SPAN, SPAN), 0)
    cols = iota2((SPAN, SPAN), 1)
    bias = jnp.where((doc == doc_row) & (rows >= cols), 0.0, NEG)
    b_blk = b_ref[...]
    c_blk = c_ref[...]
    affinity = mm_nt(c_blk, b_blk)
    old = state[...]
    old_low = old.astype(bf16)
    states_ref[0] = old_low
    from_state = mm(c_blk, old_low) * split_mm(carried, spread)
    for pair in range(PAIRS):
        lo, hi = pair * SPAN, (pair + 1) * SPAN
        mats = []
        for h in (2 * pair, 2 * pair + 1):
            decay = jnp.exp(cum[:, h : h + 1] - cum_t[h : h + 1, :] + bias)
            mats.append((affinity * decay * st_t[h : h + 1, :]).astype(bf16))
        inside = mm(jnp.concatenate(mats, axis=1), split_pair(x_ref[:, lo:hi]))
        y_ref[:, lo:hi] = inside + from_state[:, lo:hi]
    tail = split_mm(gap * st, spread)
    pushed = (x_ref[...].astype(f32) * tail).astype(bf16)
    state[...] = old * split_mm(keep, spread)[0:1, :] + mm_tn(b_blk, pushed)


def scan_bwd_kernel(
    x_ref, b_ref, c_ref, ld_ref, st_ref, states_ref, dy_ref,
    dx_ref, db_ref, dc_ref, dst_ref, dld_ref, dstate, grow, gcol,
):
    spread = head_spread()
    gather = head_gather()

    @pl.when(pl.program_id(0) == 0)
    def _():
        dstate[...] = jnp.zeros_like(dstate)
        grow[...] = jnp.zeros_like(grow)
        gcol[...] = jnp.zeros_like(gcol)

    st, cum, cum_t, st_t, doc, doc_row, carried, gap, keep = block_terms(ld_ref, st_ref, spread)
    rows = iota2((SPAN, SPAN), 0)
    cols = iota2((SPAN, SPAN), 1)
    bias = jnp.where((doc == doc_row) & (cols >= rows), 0.0, NEG)
    b_blk = b_ref[...]
    c_blk = c_ref[...]
    x_blk = x_ref[...]
    dy = dy_ref[...]
    dy_low = dy.astype(bf16)
    affinity = mm_nt(b_blk, c_blk)
    old_low = states_ref[0]
    d_new = dstate[...]
    d_new_low = d_new.astype(bf16)
    carried_wide = split_mm(carried, spread)
    tail_wide = split_mm(gap * st, spread)
    keep_wide = split_mm(keep, spread)[0:1, :]
    from_tail = mm(b_blk, d_new_low)
    d_aff = jnp.zeros((SPAN, SPAN), f32)
    for pair in range(PAIRS):
        lo, hi = pair * SPAN, (pair + 1) * SPAN
        d_mats = mm_nt(split_pair(x_blk[:, lo:hi]), dy_low[:, lo:hi])
        mats = []
        for which, h in enumerate((2 * pair, 2 * pair + 1)):
            step = st[:, h : h + 1]
            decay = jnp.exp(cum_t[h : h + 1, :] - cum[:, h : h + 1] + bias)
            scaled = affinity * decay
            mats.append((scaled * step).astype(bf16))
            d_mat = d_mats[which * SPAN : (which + 1) * SPAN, :]
            d_aff = d_aff + d_mat * decay * step
            products = d_mat * scaled
            gcol[:, h : h + 1] = jnp.sum(products, axis=1, keepdims=True)
            grow[h : h + 1, :] = jnp.sum(products * step, axis=0, keepdims=True)
        inside = mm(jnp.concatenate(mats, axis=1), split_pair(dy_low[:, lo:hi]))
        dx_ref[:, lo:hi] = inside + from_tail[:, lo:hi] * tail_wide[:, lo:hi]
    flowing = dy * carried_wide
    flowing_low = flowing.astype(bf16)
    d_cum = split_mm(flowing * mm(c_blk, old_low), gather)
    d_tail = split_mm(x_blk.astype(f32) * from_tail, gather)
    moved = d_tail * gap * st
    d_keep = jnp.sum(d_new * old_low.astype(f32), axis=0, keepdims=True)
    d_keep = split_mm(jnp.broadcast_to(d_keep, (8, D_SSM)), gather) * keep
    at_end = jnp.sum(moved, axis=0, keepdims=True) + d_keep[0:1, :]
    d_cum = d_cum - moved + grow[...].T - gcol[...] * st
    d_cum = d_cum + jnp.where(rows == SPAN - 1, at_end, 0.0)
    dst_ref[...] = gcol[...] + d_tail * gap
    dld_ref[...] = exact_mm(jnp.where(cols >= rows, 1.0, 0.0), d_cum)
    d_aff_low = d_aff.astype(bf16)
    pushed = (x_blk.astype(f32) * tail_wide).astype(bf16)
    dc_ref[...] = mm_tn(d_aff_low, b_blk) + mm_nt(flowing_low, old_low)
    db_ref[...] = mm(d_aff_low, c_blk) + mm_nt(pushed, d_new_low)
    dstate[...] = d_new * keep_wide + mm_tn(c_blk, flowing_low)


def scan_fwd(act_low, ld, st):
    length = act_low.shape[0]
    blocks = length // SPAN
    return pl.pallas_call(
        scan_fwd_kernel,
        grid=(blocks,),
        in_specs=[
            pl.BlockSpec((SPAN, D_SSM), lambda i: (i, 0)),
            pl.BlockSpec((SPAN, STATE), lambda i: (i, D_SSM // STATE)),
            pl.BlockSpec((SPAN, STATE), lambda i: (i, D_SSM // STATE + 1)),
            pl.BlockSpec((SPAN, 128), lambda i: (i, 0)),
            pl.BlockSpec((SPAN, 128), lambda i: (i, 0)),
        ],
        out_specs=[
            pl.BlockSpec((SPAN, D_SSM), lambda i: (i, 0)),
            pl.BlockSpec((1, STATE, D_SSM), lambda i: (i, 0, 0)),
        ],
        out_shape=[
            jax.ShapeDtypeStruct((length, D_SSM), f32),
            jax.ShapeDtypeStruct((blocks, STATE, D_SSM), bf16),
        ],
        scratch_shapes=[pltpu.VMEM((STATE, D_SSM), f32)],
        compiler_params=pltpu.CompilerParams(vmem_limit_bytes=40 * 2**20),
    )(act_low, act_low, act_low, ld, st)


def scan_bwd(act_low, ld, st, states, dy):
    length = act_low.shape[0]
    blocks = length // SPAN
    end = blocks - 1
    return pl.pallas_call(
        scan_bwd_kernel,
        grid=(blocks,),
        in_specs=[
            pl.BlockSpec((SPAN, D_SSM), lambda i: (end - i, 0)),
            pl.BlockSpec((SPAN, STATE), lambda i: (end - i, D_SSM // STATE)),
            pl.BlockSpec((SPAN, STATE), lambda i: (end - i, D_SSM // STATE + 1)),
            pl.BlockSpec((SPAN, 128), lambda i: (end - i, 0)),
            pl.BlockSpec((SPAN, 128), lambda i: (end - i, 0)),
            pl.BlockSpec((1, STATE, D_SSM), lambda i: (end - i, 0, 0)),
            pl.BlockSpec((SPAN, D_SSM), lambda i: (end - i, 0)),
        ],
        out_specs=[
            pl.BlockSpec((SPAN, D_SSM), lambda i: (end - i, 0)),
            pl.BlockSpec((SPAN, STATE), lambda i: (end - i, 0)),
            pl.BlockSpec((SPAN, STATE), lambda i: (end - i, 0)),
            pl.BlockSpec((SPAN, 128), lambda i: (end - i, 0)),
            pl.BlockSpec((SPAN, 128), lambda i: (end - i, 0)),
        ],
        out_shape=[
            jax.ShapeDtypeStruct((length, D_SSM), f32),
            jax.ShapeDtypeStruct((length, STATE), f32),
            jax.ShapeDtypeStruct((length, STATE), f32),
            jax.ShapeDtypeStruct((length, 128), f32),
            jax.ShapeDtypeStruct((length, 128), f32),
        ],
        scratch_shapes=[
            pltpu.VMEM((STATE, D_SSM), f32),
            pltpu.VMEM((SPAN, SPAN), f32),
            pltpu.VMEM((SPAN, SPAN), f32),
        ],
        compiler_params=pltpu.CompilerParams(vmem_limit_bytes=40 * 2**20),
    )(act_low, act_low, act_low, ld, st, states, dy)


def key_span(block):
    return max(0, block * QROWS - REACH), (block + 1) * QROWS


def fill_bias(doc_col_ref, doc_row_ref, bias, blocks):
    for block in range(blocks):
        k0, k1 = key_span(block)
        q0, q1 = block * QROWS, (block + 1) * QROWS
        shape = (k1 - k0, QROWS)
        allowed = (doc_col_ref[k0:k1, :] == doc_row_ref[:, q0:q1]) & (
            iota2(shape, 0) + k0 <= iota2(shape, 1) + q0
        )
        bias[block, 0 : k1 - k0, :] = jnp.where(allowed, 0.0, NEG)


def attend_fwd_kernel(q_ref, k_ref, v_ref, doc_col_ref, doc_row_ref, out_ref, lse_ref, bias):
    blocks = q_ref.shape[0] // QROWS

    @pl.when(pl.program_id(0) == 0)
    def _():
        fill_bias(doc_col_ref, doc_row_ref, bias, blocks)

    for block in range(blocks):
        k0, k1 = key_span(block)
        q0, q1 = block * QROWS, (block + 1) * QROWS
        scores = mm_nt(k_ref[k0:k1, :], q_ref[q0:q1, :]) * HEAD_DIM ** (-0.5)
        scores = scores + bias[block, 0 : k1 - k0, :]
        top = jnp.max(scores, axis=0, keepdims=True)
        exponent = jnp.exp(scores - top)
        total = jnp.sum(exponent, axis=0, keepdims=True)
        probability = (exponent * (1.0 / total)).astype(bf16)
        out_ref[q0:q1, :] = mm_tn(v_ref[k0:k1, :], probability).T.astype(bf16)
        lse_ref[0, :, q0:q1] = top + jnp.log(total)


def attend_bwd_kernel(
    q_ref, k_ref, v_ref, do_ref, lse_ref, doc_col_ref, doc_row_ref, dq_ref, dk_ref, dv_ref, bias
):
    blocks = q_ref.shape[0] // QROWS

    @pl.when((pl.program_id(0) == 0) & (pl.program_id(1) == 0))
    def _():
        fill_bias(doc_col_ref, doc_row_ref, bias, blocks)

    @pl.when(pl.program_id(1) == 0)
    def _():
        dk_ref[...] = jnp.zeros_like(dk_ref)
        dv_ref[...] = jnp.zeros_like(dv_ref)

    for block in range(blocks):
        k0, k1 = key_span(block)
        q0, q1 = block * QROWS, (block + 1) * QROWS
        query = q_ref[q0:q1, :]
        key = k_ref[k0:k1, :]
        d_out = do_ref[q0:q1, :].astype(bf16)
        scores = mm_nt(key, query) * HEAD_DIM ** (-0.5) + bias[block, 0 : k1 - k0, :]
        probability = jnp.exp(scores - lse_ref[0, :, q0:q1])
        dv_ref[k0:k1, :] += mm(probability.astype(bf16), d_out)
        d_prob = mm_nt(v_ref[k0:k1, :], d_out)
        delta = jnp.sum(probability * d_prob, axis=0, keepdims=True)
        d_scores = (probability * (d_prob - delta) * HEAD_DIM ** (-0.5)).astype(bf16)
        dk_ref[k0:k1, :] += mm(d_scores, query)
        dq_ref[q0:q1, :] = mm_tn(key, d_scores).T


def attend_fwd(query, key, value, doc_col, doc_row):
    length = query.shape[0]
    group = HEADS // KV_HEADS
    blocks = length // QROWS
    return pl.pallas_call(
        attend_fwd_kernel,
        grid=(HEADS,),
        in_specs=[
            pl.BlockSpec((length, HEAD_DIM), lambda h: (0, h)),
            pl.BlockSpec((length, HEAD_DIM), lambda h: (0, h // group)),
            pl.BlockSpec((length, HEAD_DIM), lambda h: (0, h // group)),
            pl.BlockSpec((length, 1), lambda h: (0, 0)),
            pl.BlockSpec((1, length), lambda h: (0, 0)),
        ],
        out_specs=[
            pl.BlockSpec((length, HEAD_DIM), lambda h: (0, h)),
            pl.BlockSpec((1, 1, length), lambda h: (h, 0, 0)),
        ],
        out_shape=[
            jax.ShapeDtypeStruct((length, HEADS * HEAD_DIM), bf16),
            jax.ShapeDtypeStruct((HEADS, 1, length), f32),
        ],
        scratch_shapes=[pltpu.VMEM((blocks, QROWS + REACH, QROWS), f32)],
        compiler_params=pltpu.CompilerParams(vmem_limit_bytes=40 * 2**20),
    )(query, key, value, doc_col, doc_row)


def attend_bwd(query, key, value, d_out, lse, doc_col, doc_row):
    length = query.shape[0]
    group = HEADS // KV_HEADS
    blocks = length // QROWS
    per_query = pl.BlockSpec((length, HEAD_DIM), lambda g, r: (0, g * group + r))
    per_key = pl.BlockSpec((length, HEAD_DIM), lambda g, r: (0, g))
    return pl.pallas_call(
        attend_bwd_kernel,
        grid=(KV_HEADS, group),
        in_specs=[
            per_query,
            per_key,
            per_key,
            per_query,
            pl.BlockSpec((1, 1, length), lambda g, r: (g * group + r, 0, 0)),
            pl.BlockSpec((length, 1), lambda g, r: (0, 0)),
            pl.BlockSpec((1, length), lambda g, r: (0, 0)),
        ],
        out_specs=[per_query, per_key, per_key],
        out_shape=[
            jax.ShapeDtypeStruct((length, HEADS * HEAD_DIM), f32),
            jax.ShapeDtypeStruct((length, KV_HEADS * HEAD_DIM), f32),
            jax.ShapeDtypeStruct((length, KV_HEADS * HEAD_DIM), f32),
        ],
        scratch_shapes=[pltpu.VMEM((blocks, QROWS + REACH, QROWS), f32)],
        compiler_params=pltpu.CompilerParams(vmem_limit_bytes=40 * 2**20),
    )(query, key, value, d_out, lse, doc_col, doc_row)


def inv_norm(values):
    return lax.rsqrt(jnp.mean(values * values, axis=-1, keepdims=True) + eps)


def norm_back(normed_grad, gain, values, inv):
    unit = values * inv
    scaled = normed_grad * gain
    back = inv * (scaled - unit * jnp.mean(scaled * unit, axis=-1, keepdims=True))
    return back, jnp.sum(normed_grad * unit, axis=0)


def angles(length):
    half_dim = HEAD_DIM // 2
    frequency = rope_base ** (-jnp.arange(half_dim, dtype=f32) / half_dim)
    table = jnp.arange(length).astype(f32)[:, None] * frequency[None, :]
    return jnp.cos(table), jnp.sin(table)


def turn(values, cosine, sine):
    length, width = values.shape
    heads = values.reshape(length, width // HEAD_DIM, HEAD_DIM)
    front, back = jnp.split(heads, 2, axis=-1)
    cosine, sine = cosine[:, None, :], sine[:, None, :]
    turned = jnp.concatenate([front * cosine - back * sine, back * cosine + front * sine], axis=-1)
    return turned.reshape(length, width)


def silu_slope(values):
    gate = jax.nn.sigmoid(values)
    return gate * (1.0 + values * (1.0 - gate))


def same_doc(doc_ids, offset):
    earlier = jnp.pad(doc_ids, (offset, 0), constant_values=-1)[: doc_ids.shape[0]]
    return (earlier == doc_ids)[:, None]


def flip(values, bit):
    places = lax.axis_size(AXES)
    return lax.ppermute(values, AXES, [(i, i ^ bit) for i in range(places)])


def add(left, right):
    return (left.astype(f32) + right.astype(f32)).astype(bf16)


def at(values, index, axis):
    return lax.dynamic_index_in_dim(values, index, axis, keepdims=False)


def scatter_steps(grads):
    dp = lax.axis_size("dp")
    chips = lax.axis_size("fsdp") // 2
    if dp != 2 or chips < 4:
        return lax.psum_scatter(grads, AXES, scatter_dimension=0, tiled=True).astype(f32)
    rows, width = grads.shape
    held = rows // (4 * chips)
    place = lax.axis_index("fsdp")
    core, y, z, x = place % 2, (place // 2) % 2, place // 4, lax.axis_index("dp")
    blocks = grads.reshape(chips, 2, 2 * held, width)
    shape = (chips // 2, 2, 2, held, width)
    own = at(blocks, core, 1).reshape(shape)
    other = (yield flip(at(blocks, 1 - core, 1), 2)).reshape(shape)

    def pick(row, col):
        zero = jnp.zeros((), place.dtype)
        start, size = (zero, row, col, zero, zero), (chips // 2, 1, 1, held, width)
        return add(lax.dynamic_slice(own, start, size), lax.dynamic_slice(other, start, size))[:, 0, 0]

    def along(first):
        return jnp.stack(
            [
                pick(jnp.where(core == 0, second, first), jnp.where(core == 0, first, second))
                for second in jnp.arange(2, dtype=place.dtype)
            ]
        )

    near = jnp.where(core == 0, x, y)
    far = jnp.where(core == 0, y, x)
    places = 4 * chips
    crossing = [(i, i ^ (4 if i & 2 else 1)) for i in range(places)]
    back = [(i, i ^ (1 if i & 2 else 4)) for i in range(places)]
    sent, own = along(1 - near), along(near)
    other = yield lax.ppermute(sent, AXES, crossing)
    sent = add(at(own, 1 - far, 0), at(other, 1 - far, 0))
    own = add(at(own, far, 0), at(other, far, 0))
    other = yield lax.ppermute(sent, AXES, back)
    level = 1
    while level < chips // 2:
        shape = (-1, 2, held, width)
        mine = (z // level) % 2
        own, other = own.reshape(shape), other.reshape(shape)
        sent = add(at(own, 1 - mine, 1), at(other, 1 - mine, 1))
        own = add(at(own, mine, 1), at(other, mine, 1))
        other = yield flip(sent, 8 * level)
        level *= 2
    return (own.astype(f32) + other.astype(f32)).reshape(held, width)


class Sums:
    def __init__(self):
        self.flying, self.sums = {}, {}

    def move(self, name, steps, value):
        try:
            self.flying[name] = (steps, steps.send(value))
        except StopIteration as stop:
            self.sums[name] = stop.value
            self.flying.pop(name, None)

    def start(self, name, grads):
        self.move(name, scatter_steps(grads.astype(bf16)), None)

    def step(self, anchor, *names):
        names = [name for name in (names or tuple(self.flying)) if name in self.flying]
        anchor, arrived = lax.optimization_barrier(
            (anchor, tuple(self.flying[name][1] for name in names))
        )
        for name, value in zip(names, arrived):
            self.move(name, self.flying[name][0], value)
        return anchor


def sum_everywhere(values):
    bit = 1
    while bit < lax.axis_size(AXES):
        values = values + flip(values, bit)
        bit *= 2
    return values


def gather(parts):
    return lax.all_gather(jnp.concatenate(parts, axis=1), AXES, axis=0, tiled=True)


def shards(
    tokens, segments, cotangent, w_in, w_out, w_query, w_key, w_value, w_attn_out, w_gate, w_up,
    w_down, norm_in, conv_weight, conv_bias, dt_bias, a_log, skip_gain, norm_gated, norm_mid,
):
    length = tokens.shape[1]
    blocks = length // SPAN
    conv_end = D_SSM + CONV_CH
    rows_held = w_in.shape[0]
    dt_pad = jnp.zeros((rows_held, 128 - M_HEADS), bf16)
    w_first = gather(
        (w_in[:, :D_SSM], w_query, w_key, w_value, w_in[:, D_SSM:conv_end], w_in[:, conv_end:], dt_pad)
    )
    w_later = gather((w_attn_out.T, w_out.T, w_gate, w_up, w_down.T))
    second_end = w_attn_out.shape[0] + w_out.shape[0]
    third_end = second_end + 2 * w_gate.shape[1]
    w_second = w_later[:, :second_end]
    w_third = w_later[:, second_end:third_end]
    w_fourth = w_later[:, third_end:]

    stream = tokens[0].astype(f32)
    doc_ids = segments[0]
    cot = cotangent[0]

    inv_in = inv_norm(stream)
    normed = (stream * inv_in * norm_in).astype(bf16)
    proj = mm(normed, w_first)
    z_gate = proj[:, :D_SSM]
    q_at, k_at, v_at = D_SSM, D_SSM + HEADS * HEAD_DIM, D_SSM + (HEADS + KV_HEADS) * HEAD_DIM
    conv_at = D_SSM + QKV
    dt_at = conv_at + CONV_CH
    conv_in = proj[:, conv_at:dt_at]
    cosine, sine = angles(length)
    query = turn(proj[:, q_at:k_at], cosine, sine).astype(bf16)
    key = turn(proj[:, k_at:v_at], cosine, sine).astype(bf16)
    value = proj[:, v_at:conv_at].astype(bf16)
    doc_float = doc_ids.astype(f32)
    doc_col, doc_row = doc_float[:, None], doc_float[None, :]
    attended, lse = attend_fwd(query, key, value, doc_col, doc_row)

    taps = conv_weight.shape[0]
    convolved = conv_bias[None, :] + conv_weight[0][None, :] * conv_in
    for offset in range(1, taps):
        shifted = jnp.pad(conv_in, ((offset, 0), (0, 0)))[:length]
        convolved = convolved + jnp.where(
            same_doc(doc_ids, offset), conv_weight[offset][None, :] * shifted, 0.0
        )
    act_low = jax.nn.silu(convolved).astype(bf16)
    x_heads = act_low[:, :D_SSM]
    raw = proj[:, dt_at : dt_at + M_HEADS] + dt_bias
    step_size = jax.nn.softplus(raw)
    log_decay = -step_size * jnp.exp(a_log)
    doc_blocks = doc_float.reshape(blocks, SPAN)
    last = doc_blocks[:, -1]
    prior = jnp.concatenate([jnp.full((1,), -1.0, f32), last[:-1]])
    wide_last = jnp.repeat(last, SPAN)[:, None]
    wide_prior = jnp.repeat(prior, SPAN)[:, None]
    ld = jnp.pad(log_decay, ((0, 0), (0, 128 - M_HEADS)))
    st = jnp.concatenate(
        [step_size, jnp.zeros((length, 125 - M_HEADS), f32), wide_last, wide_prior, doc_col], axis=1
    )
    scanned, states = scan_fwd(act_low, ld, st)
    skip_wide = jnp.repeat(skip_gain, M_HDIM)[None, :]
    ssm_out = scanned + skip_wide * x_heads.astype(f32)
    mixed_in = ssm_out * jax.nn.silu(z_gate)
    inv_gated = inv_norm(mixed_in)
    gated = (mixed_in * inv_gated * norm_gated).astype(bf16)
    branches = jnp.concatenate([attended, gated], axis=1)
    resid = stream + mm_nt(branches, w_second)
    inv_mid = inv_norm(resid)
    mid_in = (resid * inv_mid * norm_mid).astype(bf16)
    both = mm(mid_in, w_third)
    hidden_units = both.shape[1] // 2
    gate, up = both[:, :hidden_units], both[:, hidden_units:]
    hidden = (jax.nn.silu(gate) * up).astype(bf16)
    mixed = (resid + mm_nt(hidden, w_fourth)).astype(bf16)

    sums = Sums()
    d_hidden = mm(cot, w_fourth)
    sums.start("fourth", mm_tn(cot, hidden))
    d_both = jnp.concatenate(
        [(d_hidden * up * silu_slope(gate)).astype(bf16), (d_hidden * jax.nn.silu(gate)).astype(bf16)],
        axis=1,
    )
    d_both = sums.step(d_both)
    sums.start("third", mm_tn(mid_in, d_both))
    d_mid = sums.step(mm_nt(d_both, w_third), "fourth")
    back, g_norm_mid = norm_back(d_mid, norm_mid, resid, inv_mid)
    d_resid = sums.step(cot.astype(f32) + back)
    d_resid_low = d_resid.astype(bf16)
    sums.start("second", mm_tn(d_resid_low, branches))
    d_branches = sums.step(mm(d_resid_low, w_second))
    attn_width = HEADS * HEAD_DIM
    d_query, d_key, d_value = attend_bwd(
        query, key, value, d_branches[:, :attn_width], lse, doc_col, doc_row
    )
    d_query, d_branches = sums.step((d_query, d_branches))
    d_mixed_in, g_norm_gated = norm_back(d_branches[:, attn_width:], norm_gated, mixed_in, inv_gated)
    d_ssm = d_mixed_in * jax.nn.silu(z_gate)
    d_first = jnp.concatenate(
        [
            (d_mixed_in * ssm_out * silu_slope(z_gate)).astype(bf16),
            turn(d_query, cosine, -sine).astype(bf16),
            turn(d_key, cosine, -sine).astype(bf16),
            d_value.astype(bf16),
        ],
        axis=1,
    )
    d_ssm, d_first = sums.step((d_ssm, d_first))
    sums.start("first", mm_tn(normed, d_first))
    g_skip = jnp.sum(jnp.sum(d_ssm * x_heads.astype(f32), axis=0).reshape(M_HEADS, M_HDIM), axis=1)
    d_x, d_b, d_c, d_st, d_ld = scan_bwd(act_low, ld, st, states, d_ssm)
    d_x = sums.step(d_x)
    d_act = jnp.concatenate([d_x + skip_wide * d_ssm, d_b, d_c], axis=1)
    d_conv = d_act * silu_slope(convolved)
    g_conv_bias = jnp.sum(d_conv, axis=0)
    d_conv_in = conv_weight[0][None, :] * d_conv
    g_taps = [jnp.sum(d_conv * conv_in, axis=0)]
    for offset in range(1, taps):
        masked = jnp.where(same_doc(doc_ids, offset), d_conv, 0.0)
        shifted = jnp.pad(conv_in, ((offset, 0), (0, 0)))[:length]
        g_taps.append(jnp.sum(masked * shifted, axis=0))
        later = jnp.pad(masked, ((0, offset), (0, 0)))[offset:]
        d_conv_in = d_conv_in + conv_weight[offset][None, :] * later
    d_conv_in = sums.step(d_conv_in)
    g_conv_weight = jnp.stack(g_taps)
    d_ld = d_ld[:, :M_HEADS]
    d_step = d_st[:, :M_HEADS] - d_ld * jnp.exp(a_log)
    g_a_log = jnp.sum(d_ld * log_decay, axis=0)
    d_raw = d_step * jax.nn.sigmoid(raw)
    g_dt_bias = jnp.sum(d_raw, axis=0)
    d_last = jnp.concatenate(
        [d_conv_in.astype(bf16), jnp.pad(d_raw, ((0, 0), (0, 128 - M_HEADS))).astype(bf16)], axis=1
    )
    sums.start("last", mm_tn(normed, d_last))
    d_normed = sums.step(mm_nt(d_first, w_first[:, :conv_at]))
    d_normed = sums.step(d_normed + mm_nt(d_last, w_first[:, conv_at:]))
    back, g_norm_in = norm_back(d_normed, norm_in, stream, inv_in)
    grad_tokens = sums.step(d_resid + back)
    while sums.flying:
        sums.step(())
    sum_first, sum_last = sums.sums["first"], sums.sums["last"]
    sum_second, sum_third, sum_fourth = sums.sums["second"], sums.sums["third"], sums.sums["fourth"]

    small = (
        g_norm_in, g_conv_weight, g_conv_bias, g_dt_bias, g_a_log, g_skip, g_norm_gated, g_norm_mid
    )
    flat = jnp.concatenate([member.reshape(-1) for member in small])
    flat = sum_everywhere(jnp.pad(flat, (0, -flat.shape[0] % 1024)).reshape(-1, 128)).reshape(-1)
    totals, at = [], 0
    for member in small:
        totals.append(flat[at : at + member.size].reshape(member.shape))
        at += member.size

    g_w_in = jnp.concatenate([sum_first[:, :D_SSM], sum_last[:, : CONV_CH + M_HEADS]], axis=1)
    return (
        mixed[None],
        grad_tokens[None],
        g_w_in,
        sum_second[:, attn_width:].T,
        sum_first[:, q_at:k_at],
        sum_first[:, k_at:v_at],
        sum_first[:, v_at:],
        sum_second[:, :attn_width].T,
        sum_third[:, :hidden_units],
        sum_third[:, hidden_units:],
        sum_fourth.T,
    ) + tuple(totals)


def solution(mesh):
    rows = P(AXES, None)
    cols = P(None, AXES)
    whole = P(AXES, None, None)
    weights = (rows, cols, rows, rows, rows, cols, rows, rows, cols)
    in_specs = (whole, rows, whole) + weights + (P(),) * 8
    out_specs = (whole, whole) + weights + (P(),) * 8
    return jax.shard_map(shards, mesh=mesh, in_specs=in_specs, out_specs=out_specs, check_vma=False)
```

```python
from functools import partial

import jax
import jax.numpy as jnp
from jax import lax
from jax.experimental import pallas as pl
from jax.experimental.pallas import tpu as pltpu
from jax.sharding import PartitionSpec as P

HEADS = 8
KV_HEADS = 2
HEAD_DIM = 128
M_HEADS = 24
M_HDIM = 64
STATE = 128
SPAN = 128
D_SSM = 1536
CONV_CH = 1792
QKV = (HEADS + 2 * KV_HEADS) * HEAD_DIM
PAIRS = M_HEADS // 2
QROWS = 256
REACH = 512

AXES = ("fsdp", "dp")
bf16 = jnp.bfloat16
f32 = jnp.float32
eps = 1e-06
rope_base = 100000000000.0
NEG = -1e30

NT = (((1,), (1,)), ((), ()))
TN = (((0,), (0,)), ((), ()))


def mm(left, right):
    return jnp.dot(left, right, preferred_element_type=f32)


def mm_nt(left, right):
    return lax.dot_general(left, right, NT, preferred_element_type=f32)


def mm_tn(left, right):
    return lax.dot_general(left, right, TN, preferred_element_type=f32)


def exact_mm(left, right):
    return jnp.dot(left, right, precision=lax.Precision.HIGHEST, preferred_element_type=f32)


def split_mm(value, selector):
    high = value.astype(bf16)
    low = (value - high.astype(f32)).astype(bf16)
    return mm(high, selector) + mm(low, selector)


def iota2(shape, axis):
    return lax.broadcasted_iota(jnp.int32, shape, axis)


def head_spread():
    rows = iota2((SPAN, D_SSM), 0)
    cols = iota2((SPAN, D_SSM), 1)
    return jnp.where(cols // M_HDIM == rows, 1.0, 0.0).astype(bf16)


def head_gather():
    rows = iota2((D_SSM, SPAN), 0)
    cols = iota2((D_SSM, SPAN), 1)
    return jnp.where(rows // M_HDIM == cols, 1.0, 0.0).astype(bf16)


def split_pair(block):
    lanes = iota2(block.shape, 1)
    zero = jnp.zeros_like(block)
    return jnp.concatenate(
        [jnp.where(lanes < M_HDIM, block, zero), jnp.where(lanes < M_HDIM, zero, block)], axis=0
    )


def block_terms(ld_ref, st_ref, spread):
    ld = ld_ref[...]
    st = st_ref[...]
    rows = iota2((SPAN, SPAN), 0)
    cols = iota2((SPAN, SPAN), 1)
    cum = exact_mm(jnp.where(rows >= cols, 1.0, 0.0), ld)
    cum_t = cum.T
    st_t = st.T
    doc = st[:, 127:128]
    prior = st[:, 126:127]
    last = st[:, 125:126]
    doc_row = st_t[127:128, :]
    carried = jnp.where(doc == prior, jnp.exp(cum), 0.0)
    gap = jnp.where(doc == last, jnp.exp(cum[SPAN - 1 : SPAN, :] - cum), 0.0)
    keep = jnp.where(last == prior, jnp.exp(cum[SPAN - 1 : SPAN, :]), 0.0)
    keep = keep[0:8, :]
    return (st, cum, cum_t, st_t, doc, doc_row, carried, gap, keep)


def scan_fwd_kernel(x_ref, b_ref, c_ref, ld_ref, st_ref, y_ref, states_ref, state):
    spread = head_spread()

    @pl.when(pl.program_id(0) == 0)
    def _():
        state[...] = jnp.zeros_like(state)

    st, cum, cum_t, st_t, doc, doc_row, carried, gap, keep = block_terms(ld_ref, st_ref, spread)
    rows = iota2((SPAN, SPAN), 0)
    cols = iota2((SPAN, SPAN), 1)
    bias = jnp.where((doc == doc_row) & (rows >= cols), 0.0, NEG)
    b_blk = b_ref[...]
    c_blk = c_ref[...]
    affinity = mm_nt(c_blk, b_blk)
    old = state[...]
    old_low = old.astype(bf16)
    states_ref[0] = old_low
    from_state = mm(c_blk, old_low) * split_mm(carried, spread)
    for pair in range(PAIRS):
        lo, hi = pair * SPAN, (pair + 1) * SPAN
        mats = []
        for h in (2 * pair, 2 * pair + 1):
            decay = jnp.exp(cum[:, h : h + 1] - cum_t[h : h + 1, :] + bias)
            mats.append((affinity * decay * st_t[h : h + 1, :]).astype(bf16))
        inside = mm(jnp.concatenate(mats, axis=1), split_pair(x_ref[:, lo:hi]))
        y_ref[:, lo:hi] = inside + from_state[:, lo:hi]
    tail = split_mm(gap * st, spread)
    pushed = (x_ref[...].astype(f32) * tail).astype(bf16)
    state[...] = old * split_mm(keep, spread)[0:1, :] + mm_tn(b_blk, pushed)


def scan_bwd_kernel(
    x_ref, b_ref, c_ref, ld_ref, st_ref, states_ref, dy_ref, skip_ref,
    dx_ref, dst_ref, dld_ref, dskip_ref, dstate, grow, gcol,
):
    spread = head_spread()
    gather = head_gather()

    @pl.when(pl.program_id(0) == 0)
    def _():
        dstate[...] = jnp.zeros_like(dstate)
        grow[...] = jnp.zeros_like(grow)
        gcol[...] = jnp.zeros_like(gcol)
        dskip_ref[...] = jnp.zeros_like(dskip_ref)

    st, cum, cum_t, st_t, doc, doc_row, carried, gap, keep = block_terms(ld_ref, st_ref, spread)
    rows = iota2((SPAN, SPAN), 0)
    cols = iota2((SPAN, SPAN), 1)
    bias = jnp.where((doc == doc_row) & (cols >= rows), 0.0, NEG)
    b_blk = b_ref[...]
    c_blk = c_ref[...]
    x_blk = x_ref[...]
    dy = dy_ref[...]
    dy_low = dy.astype(bf16)
    affinity = mm_nt(b_blk, c_blk)
    old_low = states_ref[0]
    d_new = dstate[...]
    d_new_low = d_new.astype(bf16)
    carried_wide = split_mm(carried, spread)
    tail_wide = split_mm(gap * st, spread)
    keep_wide = split_mm(keep, spread)[0:1, :]
    from_tail = mm(b_blk, d_new_low)
    d_aff = jnp.zeros((SPAN, SPAN), f32)
    for pair in range(PAIRS):
        lo, hi = pair * SPAN, (pair + 1) * SPAN
        d_mats = mm_nt(split_pair(x_blk[:, lo:hi]), dy_low[:, lo:hi])
        mats = []
        for which, h in enumerate((2 * pair, 2 * pair + 1)):
            step = st[:, h : h + 1]
            decay = jnp.exp(cum_t[h : h + 1, :] - cum[:, h : h + 1] + bias)
            scaled = affinity * decay
            mats.append((scaled * step).astype(bf16))
            d_mat = d_mats[which * SPAN : (which + 1) * SPAN, :]
            d_aff = d_aff + d_mat * decay * step
            products = d_mat * scaled
            gcol[:, h : h + 1] = jnp.sum(products, axis=1, keepdims=True)
            grow[h : h + 1, :] = jnp.sum(products * step, axis=0, keepdims=True)
        inside = mm(jnp.concatenate(mats, axis=1), split_pair(dy_low[:, lo:hi]))
        inside = inside + skip_ref[:, lo:hi] * dy[:, lo:hi]
        dx_ref[:, lo:hi] = inside + from_tail[:, lo:hi] * tail_wide[:, lo:hi]
    dskip_ref[0:1, :] += jnp.sum(dy * x_blk.astype(f32), axis=0, keepdims=True)
    flowing = dy * carried_wide
    flowing_low = flowing.astype(bf16)
    d_cum = split_mm(flowing * mm(c_blk, old_low), gather)
    d_tail = split_mm(x_blk.astype(f32) * from_tail, gather)
    moved = d_tail * gap * st
    d_keep = jnp.sum(d_new * old_low.astype(f32), axis=0, keepdims=True)
    d_keep = split_mm(jnp.broadcast_to(d_keep, (8, D_SSM)), gather) * keep
    at_end = jnp.sum(moved, axis=0, keepdims=True) + d_keep[0:1, :]
    d_cum = d_cum - moved + grow[...].T - gcol[...] * st
    d_cum = d_cum + jnp.where(rows == SPAN - 1, at_end, 0.0)
    dst_ref[...] = gcol[...] + d_tail * gap
    dld_ref[...] = exact_mm(jnp.where(cols >= rows, 1.0, 0.0), d_cum)
    d_aff_low = d_aff.astype(bf16)
    pushed = (x_blk.astype(f32) * tail_wide).astype(bf16)
    dx_ref[:, D_SSM + STATE :] = mm_tn(d_aff_low, b_blk) + mm_nt(flowing_low, old_low)
    dx_ref[:, D_SSM : D_SSM + STATE] = mm(d_aff_low, c_blk) + mm_nt(pushed, d_new_low)
    dstate[...] = d_new * keep_wide + mm_tn(c_blk, flowing_low)


def scan_fwd(act_low, ld, st):
    length = act_low.shape[0]
    blocks = length // SPAN
    return pl.pallas_call(
        scan_fwd_kernel,
        grid=(blocks,),
        in_specs=[
            pl.BlockSpec((SPAN, D_SSM), lambda i: (i, 0)),
            pl.BlockSpec((SPAN, STATE), lambda i: (i, D_SSM // STATE)),
            pl.BlockSpec((SPAN, STATE), lambda i: (i, D_SSM // STATE + 1)),
            pl.BlockSpec((SPAN, 128), lambda i: (i, 0)),
            pl.BlockSpec((SPAN, 128), lambda i: (i, 0)),
        ],
        out_specs=[
            pl.BlockSpec((SPAN, D_SSM), lambda i: (i, 0)),
            pl.BlockSpec((1, STATE, D_SSM), lambda i: (i, 0, 0)),
        ],
        out_shape=[
            jax.ShapeDtypeStruct((length, D_SSM), f32),
            jax.ShapeDtypeStruct((blocks, STATE, D_SSM), bf16),
        ],
        scratch_shapes=[pltpu.VMEM((STATE, D_SSM), f32)],
        compiler_params=pltpu.CompilerParams(vmem_limit_bytes=40 * 2**20),
    )(act_low, act_low, act_low, ld, st)


def scan_bwd(act_low, ld, st, states, dy, skip):
    length = act_low.shape[0]
    blocks = length // SPAN
    end = blocks - 1
    return pl.pallas_call(
        scan_bwd_kernel,
        grid=(blocks,),
        in_specs=[
            pl.BlockSpec((SPAN, D_SSM), lambda i: (end - i, 0)),
            pl.BlockSpec((SPAN, STATE), lambda i: (end - i, D_SSM // STATE)),
            pl.BlockSpec((SPAN, STATE), lambda i: (end - i, D_SSM // STATE + 1)),
            pl.BlockSpec((SPAN, 128), lambda i: (end - i, 0)),
            pl.BlockSpec((SPAN, 128), lambda i: (end - i, 0)),
            pl.BlockSpec((1, STATE, D_SSM), lambda i: (end - i, 0, 0)),
            pl.BlockSpec((SPAN, D_SSM), lambda i: (end - i, 0)),
            pl.BlockSpec((1, D_SSM), lambda i: (0, 0)),
        ],
        out_specs=[
            pl.BlockSpec((SPAN, CONV_CH), lambda i: (end - i, 0)),
            pl.BlockSpec((SPAN, 128), lambda i: (end - i, 0)),
            pl.BlockSpec((SPAN, 128), lambda i: (end - i, 0)),
            pl.BlockSpec((8, D_SSM), lambda i: (0, 0)),
        ],
        out_shape=[
            jax.ShapeDtypeStruct((length, CONV_CH), f32),
            jax.ShapeDtypeStruct((length, 128), f32),
            jax.ShapeDtypeStruct((length, 128), f32),
            jax.ShapeDtypeStruct((8, D_SSM), f32),
        ],
        scratch_shapes=[
            pltpu.VMEM((STATE, D_SSM), f32),
            pltpu.VMEM((SPAN, SPAN), f32),
            pltpu.VMEM((SPAN, SPAN), f32),
        ],
        compiler_params=pltpu.CompilerParams(vmem_limit_bytes=40 * 2**20),
    )(act_low, act_low, act_low, ld, st, states, dy, skip)


def key_span(block):
    return max(0, block * QROWS - REACH), (block + 1) * QROWS


def fill_bias(doc_col_ref, doc_row_ref, bias, blocks):
    for block in range(blocks):
        k0, k1 = key_span(block)
        q0, q1 = block * QROWS, (block + 1) * QROWS
        shape = (k1 - k0, QROWS)
        allowed = (doc_col_ref[k0:k1, :] == doc_row_ref[:, q0:q1]) & (
            iota2(shape, 0) + k0 <= iota2(shape, 1) + q0
        )
        bias[block, 0 : k1 - k0, :] = jnp.where(allowed, 0.0, NEG)


def attend_fwd_kernel(q_ref, k_ref, v_ref, doc_col_ref, doc_row_ref, out_ref, lse_ref, bias):
    blocks = q_ref.shape[0] // QROWS

    @pl.when(pl.program_id(0) == 0)
    def _():
        fill_bias(doc_col_ref, doc_row_ref, bias, blocks)

    for block in range(blocks):
        k0, k1 = key_span(block)
        q0, q1 = block * QROWS, (block + 1) * QROWS
        scores = mm_nt(k_ref[k0:k1, :], q_ref[q0:q1, :]) * HEAD_DIM ** (-0.5)
        scores = scores + bias[block, 0 : k1 - k0, :]
        top = jnp.max(scores, axis=0, keepdims=True)
        exponent = jnp.exp(scores - top)
        total = jnp.sum(exponent, axis=0, keepdims=True)
        probability = (exponent * (1.0 / total)).astype(bf16)
        out_ref[q0:q1, :] = mm_tn(v_ref[k0:k1, :], probability).T.astype(bf16)
        lse_ref[0, :, q0:q1] = top + jnp.log(total)


def attend_bwd_kernel(
    q_ref, k_ref, v_ref, do_ref, lse_ref, doc_col_ref, doc_row_ref, dq_ref, dk_ref, dv_ref, bias
):
    blocks = q_ref.shape[0] // QROWS

    @pl.when((pl.program_id(0) == 0) & (pl.program_id(1) == 0))
    def _():
        fill_bias(doc_col_ref, doc_row_ref, bias, blocks)

    @pl.when(pl.program_id(1) == 0)
    def _():
        dk_ref[...] = jnp.zeros_like(dk_ref)
        dv_ref[...] = jnp.zeros_like(dv_ref)

    for block in range(blocks):
        k0, k1 = key_span(block)
        q0, q1 = block * QROWS, (block + 1) * QROWS
        query = q_ref[q0:q1, :]
        key = k_ref[k0:k1, :]
        d_out = do_ref[q0:q1, :].astype(bf16)
        scores = mm_nt(key, query) * HEAD_DIM ** (-0.5) + bias[block, 0 : k1 - k0, :]
        probability = jnp.exp(scores - lse_ref[0, :, q0:q1])
        dv_ref[k0:k1, :] += mm(probability.astype(bf16), d_out)
        d_prob = mm_nt(v_ref[k0:k1, :], d_out)
        delta = jnp.sum(probability * d_prob, axis=0, keepdims=True)
        d_scores = (probability * (d_prob - delta) * HEAD_DIM ** (-0.5)).astype(bf16)
        dk_ref[k0:k1, :] += mm(d_scores, query)
        dq_ref[q0:q1, :] = mm_tn(key, d_scores).T


def attend_fwd(query, key, value, doc_col, doc_row):
    length = query.shape[0]
    group = HEADS // KV_HEADS
    blocks = length // QROWS
    return pl.pallas_call(
        attend_fwd_kernel,
        grid=(HEADS,),
        in_specs=[
            pl.BlockSpec((length, HEAD_DIM), lambda h: (0, h)),
            pl.BlockSpec((length, HEAD_DIM), lambda h: (0, h // group)),
            pl.BlockSpec((length, HEAD_DIM), lambda h: (0, h // group)),
            pl.BlockSpec((length, 1), lambda h: (0, 0)),
            pl.BlockSpec((1, length), lambda h: (0, 0)),
        ],
        out_specs=[
            pl.BlockSpec((length, HEAD_DIM), lambda h: (0, h)),
            pl.BlockSpec((1, 1, length), lambda h: (h, 0, 0)),
        ],
        out_shape=[
            jax.ShapeDtypeStruct((length, HEADS * HEAD_DIM), bf16),
            jax.ShapeDtypeStruct((HEADS, 1, length), f32),
        ],
        scratch_shapes=[pltpu.VMEM((blocks, QROWS + REACH, QROWS), f32)],
        compiler_params=pltpu.CompilerParams(vmem_limit_bytes=40 * 2**20),
    )(query, key, value, doc_col, doc_row)


def attend_bwd(query, key, value, d_out, lse, doc_col, doc_row):
    length = query.shape[0]
    group = HEADS // KV_HEADS
    blocks = length // QROWS
    per_query = pl.BlockSpec((length, HEAD_DIM), lambda g, r: (0, g * group + r))
    per_key = pl.BlockSpec((length, HEAD_DIM), lambda g, r: (0, g))
    return pl.pallas_call(
        attend_bwd_kernel,
        grid=(KV_HEADS, group),
        in_specs=[
            per_query,
            per_key,
            per_key,
            per_query,
            pl.BlockSpec((1, 1, length), lambda g, r: (g * group + r, 0, 0)),
            pl.BlockSpec((length, 1), lambda g, r: (0, 0)),
            pl.BlockSpec((1, length), lambda g, r: (0, 0)),
        ],
        out_specs=[per_query, per_key, per_key],
        out_shape=[
            jax.ShapeDtypeStruct((length, HEADS * HEAD_DIM), f32),
            jax.ShapeDtypeStruct((length, KV_HEADS * HEAD_DIM), f32),
            jax.ShapeDtypeStruct((length, KV_HEADS * HEAD_DIM), f32),
        ],
        scratch_shapes=[pltpu.VMEM((blocks, QROWS + REACH, QROWS), f32)],
        compiler_params=pltpu.CompilerParams(vmem_limit_bytes=40 * 2**20),
    )(query, key, value, d_out, lse, doc_col, doc_row)


LANES = 128
CONV_BLOCKS = CONV_CH // LANES


def conv_shifts(values, mask_ref, taps):
    shifts = [values]
    for offset in range(1, taps):
        allowed = jnp.broadcast_to(mask_ref[:, offset : offset + 1], values.shape)
        shifts.append(jnp.where(allowed > 0.0, pltpu.roll(values, offset, 0), 0.0))
    return shifts


def conv_sum(shifts, weight_ref, bias_ref):
    total = bias_ref[...]
    for offset, shifted in enumerate(shifts):
        total = total + weight_ref[offset : offset + 1, :] * shifted
    return total


def conv_fwd_kernel(x_ref, mask_ref, weight_ref, bias_ref, act_ref):
    total = conv_sum(conv_shifts(x_ref[...], mask_ref, weight_ref.shape[0]), weight_ref, bias_ref)
    act_ref[...] = (total * jax.nn.sigmoid(total)).astype(bf16)


def conv_bwd_kernel(
    x_ref, d_act_ref, d_raw_ref, mask_ref, weight_ref, bias_ref, out_ref, small_ref
):
    step = pl.program_id(0)
    length = x_ref.shape[0]

    @pl.when(step == CONV_BLOCKS)
    def _():
        out_ref[...] = d_raw_ref[...]

    @pl.when(step < CONV_BLOCKS)
    def _():
        shifts = conv_shifts(x_ref[...], mask_ref, weight_ref.shape[0])
        total = conv_sum(shifts, weight_ref, bias_ref)
        gate = jax.nn.sigmoid(total)
        d_total = d_act_ref[...] * (gate * (1.0 + total * (1.0 - gate)))
        small_ref[...] = jnp.zeros_like(small_ref)
        small_ref[0:1, :] = jnp.sum(d_total, axis=0, keepdims=True)
        d_in = weight_ref[0:1, :] * d_total
        for offset, shifted in enumerate(shifts):
            small_ref[offset + 1 : offset + 2, :] = jnp.sum(d_total * shifted, axis=0, keepdims=True)
            if offset:
                allowed = jnp.broadcast_to(mask_ref[:, offset : offset + 1], d_total.shape)
                masked = jnp.where(allowed > 0.0, d_total, 0.0)
                later = pltpu.roll(masked, length - offset, 0)
                d_in = d_in + weight_ref[offset : offset + 1, :] * later
        out_ref[...] = d_in.astype(bf16)


def conv_fwd(proj, first, masks, weight, bias):
    length, taps = masks.shape
    return pl.pallas_call(
        conv_fwd_kernel,
        grid=(CONV_BLOCKS,),
        in_specs=[
            pl.BlockSpec((length, LANES), lambda i: (0, first + i)),
            pl.BlockSpec((length, taps), lambda i: (0, 0)),
            pl.BlockSpec((taps, LANES), lambda i: (0, i)),
            pl.BlockSpec((1, LANES), lambda i: (0, i)),
        ],
        out_specs=pl.BlockSpec((length, LANES), lambda i: (0, i)),
        out_shape=jax.ShapeDtypeStruct((length, CONV_CH), bf16),
        compiler_params=pltpu.CompilerParams(vmem_limit_bytes=40 * 2**20),
    )(proj, masks, weight, bias)


def conv_bwd(proj, first, d_act, d_raw, masks, weight, bias):
    length, taps = masks.shape
    end = CONV_BLOCKS - 1
    return pl.pallas_call(
        conv_bwd_kernel,
        grid=(CONV_BLOCKS + 1,),
        in_specs=[
            pl.BlockSpec((length, LANES), lambda i: (0, first + jnp.minimum(i, end))),
            pl.BlockSpec((length, LANES), lambda i: (0, jnp.minimum(i, end))),
            pl.BlockSpec((length, LANES), lambda i: (0, 0)),
            pl.BlockSpec((length, taps), lambda i: (0, 0)),
            pl.BlockSpec((taps, LANES), lambda i: (0, jnp.minimum(i, end))),
            pl.BlockSpec((1, LANES), lambda i: (0, jnp.minimum(i, end))),
        ],
        out_specs=[
            pl.BlockSpec((length, LANES), lambda i: (0, i)),
            pl.BlockSpec((8, LANES), lambda i: (0, jnp.minimum(i, end))),
        ],
        out_shape=[
            jax.ShapeDtypeStruct((length, CONV_CH + LANES), bf16),
            jax.ShapeDtypeStruct((8, CONV_CH), f32),
        ],
        compiler_params=pltpu.CompilerParams(vmem_limit_bytes=40 * 2**20),
    )(proj, d_act, d_raw, masks, weight, bias)


def units_bwd_kernel(cot_ref, down_ref, both_ref, out_ref):
    units = down_ref.shape[1]
    d_hidden = mm(cot_ref[...], down_ref[...])
    gate = both_ref[:, :units]
    sigmoid = jax.nn.sigmoid(gate)
    slope = sigmoid * (1.0 + gate * (1.0 - sigmoid))
    out_ref[:, :units] = (d_hidden * both_ref[:, units:] * slope).astype(bf16)
    out_ref[:, units:] = (d_hidden * (gate * sigmoid)).astype(bf16)


def units_bwd(cot, weights, both):
    length, width = cot.shape
    units = both.shape[1] // 2
    rows = 128
    return pl.pallas_call(
        units_bwd_kernel,
        grid=(length // rows,),
        in_specs=[
            pl.BlockSpec((rows, width), lambda i: (i, 0)),
            pl.BlockSpec((width, units), lambda i: (0, 0)),
            pl.BlockSpec((rows, 2 * units), lambda i: (i, 0)),
        ],
        out_specs=pl.BlockSpec((rows, 2 * units), lambda i: (i, 0)),
        out_shape=jax.ShapeDtypeStruct((length, 2 * units), bf16),
        compiler_params=pltpu.CompilerParams(vmem_limit_bytes=40 * 2**20),
    )(cot, weights, both)


def inv_norm(values):
    return lax.rsqrt(jnp.mean(values * values, axis=-1, keepdims=True) + eps)


def norm_back(normed_grad, gain, values, inv, tie=lambda mean: mean):
    unit = values * inv
    scaled = normed_grad * gain
    back = inv * (scaled - unit * tie(jnp.mean(scaled * unit, axis=-1, keepdims=True)))
    return back, jnp.sum(normed_grad * unit, axis=0)


def angles(length):
    half_dim = HEAD_DIM // 2
    frequency = rope_base ** (-jnp.arange(half_dim, dtype=f32) / half_dim)
    table = jnp.arange(length).astype(f32)[:, None] * frequency[None, :]
    return jnp.cos(table), jnp.sin(table)


def turn(values, cosine, sine):
    length, width = values.shape
    heads = values.reshape(length, width // HEAD_DIM, HEAD_DIM)
    front, back = jnp.split(heads, 2, axis=-1)
    cosine, sine = cosine[:, None, :], sine[:, None, :]
    turned = jnp.concatenate([front * cosine - back * sine, back * cosine + front * sine], axis=-1)
    return turned.reshape(length, width)


def silu_slope(values):
    gate = jax.nn.sigmoid(values)
    return gate * (1.0 + values * (1.0 - gate))


def same_doc(doc_ids, offset):
    earlier = jnp.pad(doc_ids, (offset, 0), constant_values=-1)[: doc_ids.shape[0]]
    return (earlier == doc_ids)[:, None]


def flip(values, bit):
    places = lax.axis_size(AXES)
    return lax.ppermute(values, AXES, [(i, i ^ bit) for i in range(places)])


def add(left, right):
    return (left.astype(f32) + right.astype(f32)).astype(bf16)


def at(values, index, axis):
    return lax.dynamic_index_in_dim(values, index, axis, keepdims=False)


def scatter_steps(grads):
    dp = lax.axis_size("dp")
    chips = lax.axis_size("fsdp") // 2
    if dp != 2 or chips < 4:
        return lax.psum_scatter(grads, AXES, scatter_dimension=0, tiled=True).astype(f32)
    rows, width = grads.shape
    held = rows // (4 * chips)
    place = lax.axis_index("fsdp")
    core, y, z, x = place % 2, (place // 2) % 2, place // 4, lax.axis_index("dp")
    blocks = grads.reshape(chips, 2, 2 * held, width)
    shape = (chips // 2, 2, 2, held, width)
    own = at(blocks, core, 1).reshape(shape)
    other = (yield flip(at(blocks, 1 - core, 1), 2)).reshape(shape)

    def pick(row, col):
        zero = jnp.zeros((), place.dtype)
        start, size = (zero, row, col, zero, zero), (chips // 2, 1, 1, held, width)
        return add(lax.dynamic_slice(own, start, size), lax.dynamic_slice(other, start, size))[:, 0, 0]

    def along(first):
        return jnp.stack(
            [
                pick(jnp.where(core == 0, second, first), jnp.where(core == 0, first, second))
                for second in jnp.arange(2, dtype=place.dtype)
            ]
        )

    near = jnp.where(core == 0, x, y)
    far = jnp.where(core == 0, y, x)
    places = 4 * chips
    crossing = [(i, i ^ (4 if i & 2 else 1)) for i in range(places)]
    back = [(i, i ^ (1 if i & 2 else 4)) for i in range(places)]
    sent, own = along(1 - near), along(near)
    other = yield lax.ppermute(sent, AXES, crossing)
    sent = add(at(own, 1 - far, 0), at(other, 1 - far, 0))
    own = add(at(own, far, 0), at(other, far, 0))
    other = yield lax.ppermute(sent, AXES, back)
    level = 1
    while level < chips // 2:
        shape = (-1, 2, held, width)
        mine = (z // level) % 2
        own, other = own.reshape(shape), other.reshape(shape)
        sent = add(at(own, 1 - mine, 1), at(other, 1 - mine, 1))
        own = add(at(own, mine, 1), at(other, mine, 1))
        other = yield flip(sent, 8 * level)
        level *= 2
    return (own.astype(f32) + other.astype(f32)).reshape(held, width)


class Sums:
    def __init__(self):
        self.flying, self.sums = {}, {}

    def move(self, name, steps, value):
        try:
            self.flying[name] = (steps, steps.send(value))
        except StopIteration as stop:
            self.sums[name] = stop.value
            self.flying.pop(name, None)

    def start(self, name, grads):
        self.move(name, scatter_steps(grads.astype(bf16)), None)

    def step(self, anchor, *names):
        names = [name for name in (names or tuple(self.flying)) if name in self.flying]
        anchor, arrived = lax.optimization_barrier(
            (anchor, tuple(self.flying[name][1] for name in names))
        )
        for name, value in zip(names, arrived):
            self.move(name, self.flying[name][0], value)
        return anchor


def sum_everywhere(values):
    bit = 1
    while bit < lax.axis_size(AXES):
        values = values + flip(values, bit)
        bit *= 2
    return values


def gather(parts):
    return lax.all_gather(jnp.concatenate(parts, axis=1), AXES, axis=0, tiled=True)


def shards(
    tokens, segments, cotangent, w_in, w_out, w_query, w_key, w_value, w_attn_out, w_gate, w_up,
    w_down, norm_in, conv_weight, conv_bias, dt_bias, a_log, skip_gain, norm_gated, norm_mid,
):
    length = tokens.shape[1]
    blocks = length // SPAN
    conv_end = D_SSM + CONV_CH
    rows_held = w_in.shape[0]
    dt_pad = jnp.zeros((rows_held, 128 - M_HEADS), bf16)
    w_first = gather(
        (w_in[:, :D_SSM], w_query, w_key, w_value, w_in[:, D_SSM:conv_end], w_in[:, conv_end:], dt_pad)
    )
    w_later = gather((w_down.T, w_gate, w_up, w_attn_out.T, w_out.T))
    fourth_end = w_down.shape[0]
    third_end = fourth_end + 2 * w_gate.shape[1]
    w_fourth = w_later[:, :fourth_end]
    w_third = w_later[:, fourth_end:third_end]
    w_second = w_later[:, third_end:]

    stream = tokens[0].astype(f32)
    doc_ids = segments[0]
    cot = cotangent[0]

    inv_in = inv_norm(stream)
    normed = (stream * inv_in * norm_in).astype(bf16)
    proj = mm(normed, w_first)
    z_gate = proj[:, :D_SSM]
    q_at, k_at, v_at = D_SSM, D_SSM + HEADS * HEAD_DIM, D_SSM + (HEADS + KV_HEADS) * HEAD_DIM
    conv_at = D_SSM + QKV
    dt_at = conv_at + CONV_CH
    cosine, sine = angles(length)
    query = turn(proj[:, q_at:k_at], cosine, sine).astype(bf16)
    key = turn(proj[:, k_at:v_at], cosine, sine).astype(bf16)
    value = proj[:, v_at:conv_at].astype(bf16)
    doc_float = doc_ids.astype(f32)
    doc_col, doc_row = doc_float[:, None], doc_float[None, :]
    attended, lse = attend_fwd(query, key, value, doc_col, doc_row)

    taps = conv_weight.shape[0]
    masks = jnp.concatenate([same_doc(doc_ids, offset) for offset in range(taps)], axis=1).astype(f32)
    conv_bias_row = conv_bias[None, :]
    act_low = conv_fwd(proj, conv_at // LANES, masks, conv_weight, conv_bias_row)
    x_heads = act_low[:, :D_SSM]
    raw = proj[:, dt_at : dt_at + M_HEADS] + dt_bias
    step_size = jax.nn.softplus(raw)
    log_decay = -step_size * jnp.exp(a_log)
    doc_blocks = doc_float.reshape(blocks, SPAN)
    last = doc_blocks[:, -1]
    prior = jnp.concatenate([jnp.full((1,), -1.0, f32), last[:-1]])
    wide_last = jnp.repeat(last, SPAN)[:, None]
    wide_prior = jnp.repeat(prior, SPAN)[:, None]
    ld = jnp.pad(log_decay, ((0, 0), (0, 128 - M_HEADS)))
    st = jnp.concatenate(
        [step_size, jnp.zeros((length, 125 - M_HEADS), f32), wide_last, wide_prior, doc_col], axis=1
    )
    scanned, states = scan_fwd(act_low, ld, st)
    skip_wide = jnp.repeat(skip_gain, M_HDIM)[None, :]
    ssm_out = scanned + skip_wide * x_heads.astype(f32)
    mixed_in = ssm_out * jax.nn.silu(z_gate)
    inv_gated = inv_norm(mixed_in)
    gated = (mixed_in * inv_gated * norm_gated).astype(bf16)
    branches = jnp.concatenate([attended, gated], axis=1)
    resid = stream + mm_nt(branches, w_second)
    inv_mid = inv_norm(resid)
    mid_in = (resid * inv_mid * norm_mid).astype(bf16)
    both = mm(mid_in, w_third)
    hidden_units = both.shape[1] // 2
    gate, up = both[:, :hidden_units], both[:, hidden_units:]
    hidden = (jax.nn.silu(gate) * up).astype(bf16)
    mixed = (resid + mm_nt(hidden, w_fourth)).astype(bf16)

    sums = Sums()
    sums.start("fourth", mm_tn(cot, hidden))
    d_both = units_bwd(cot, w_later, both)
    d_both = sums.step(d_both)
    sums.start("third", mm_tn(mid_in, d_both))
    d_mid = mm_nt(d_both, w_third)
    back, g_norm_mid = norm_back(d_mid, norm_mid, resid, inv_mid, sums.step)
    d_resid = cot.astype(f32) + back
    d_resid_low = d_resid.astype(bf16)
    sums.start("second", mm_tn(d_resid_low, branches))
    d_branches = sums.step(mm(d_resid_low, w_second), "fourth", "second")
    attn_width = HEADS * HEAD_DIM
    d_query, d_key, d_value = attend_bwd(
        query, key, value, d_branches[:, :attn_width], lse, doc_col, doc_row
    )
    d_query, d_branches = sums.step((d_query, d_branches))
    d_mixed_in, g_norm_gated = norm_back(d_branches[:, attn_width:], norm_gated, mixed_in, inv_gated)
    d_ssm = d_mixed_in * jax.nn.silu(z_gate)
    d_first = jnp.concatenate(
        [
            (d_mixed_in * ssm_out * silu_slope(z_gate)).astype(bf16),
            turn(d_query, cosine, -sine).astype(bf16),
            turn(d_key, cosine, -sine).astype(bf16),
            d_value.astype(bf16),
        ],
        axis=1,
    )
    d_ssm, d_first = sums.step((d_ssm, d_first))
    sums.start("first", mm_tn(normed, d_first))
    d_act, d_st, d_ld, g_skip_wide = scan_bwd(act_low, ld, st, states, d_ssm, skip_wide)
    g_skip = jnp.sum(g_skip_wide[0].reshape(M_HEADS, M_HDIM), axis=1)
    d_st = sums.step(d_st)
    d_ld = d_ld[:, :M_HEADS]
    d_step = d_st[:, :M_HEADS] - d_ld * jnp.exp(a_log)
    g_a_log = jnp.sum(d_ld * log_decay, axis=0)
    d_raw = d_step * jax.nn.sigmoid(raw)
    g_dt_bias = jnp.sum(d_raw, axis=0)
    d_raw_low = jnp.pad(d_raw.astype(bf16), ((0, 0), (0, LANES - M_HEADS)))
    d_last, g_conv = conv_bwd(
        proj, conv_at // LANES, d_act, d_raw_low, masks, conv_weight, conv_bias_row
    )
    g_conv_bias, g_conv_weight = g_conv[0], g_conv[1 : taps + 1]
    d_last = sums.step(d_last)
    sums.start("last", mm_tn(normed, d_last))
    d_normed = mm_nt(d_first, w_first[:, :conv_at])
    d_last = sums.step(d_last)
    d_normed = d_normed + mm_nt(d_last, w_first[:, conv_at:])
    back, g_norm_in = norm_back(d_normed, norm_in, stream, inv_in, sums.step)
    grad_tokens = d_resid + back
    while sums.flying:
        sums.step(())
    sum_first, sum_last = sums.sums["first"], sums.sums["last"]
    sum_second, sum_third, sum_fourth = sums.sums["second"], sums.sums["third"], sums.sums["fourth"]

    small = (
        g_norm_in, g_conv_weight, g_conv_bias, g_dt_bias, g_a_log, g_skip, g_norm_gated, g_norm_mid
    )
    flat = jnp.concatenate([member.reshape(-1) for member in small])
    flat = sum_everywhere(jnp.pad(flat, (0, -flat.shape[0] % 1024)).reshape(-1, 128)).reshape(-1)
    totals, at = [], 0
    for member in small:
        totals.append(flat[at : at + member.size].reshape(member.shape))
        at += member.size

    g_w_in = jnp.concatenate([sum_first[:, :D_SSM], sum_last[:, : CONV_CH + M_HEADS]], axis=1)
    return (
        mixed[None],
        grad_tokens[None],
        g_w_in,
        sum_second[:, attn_width:].T,
        sum_first[:, q_at:k_at],
        sum_first[:, k_at:v_at],
        sum_first[:, v_at:],
        sum_second[:, :attn_width].T,
        sum_third[:, :hidden_units],
        sum_third[:, hidden_units:],
        sum_fourth.T,
    ) + tuple(totals)


def solution(mesh):
    rows = P(AXES, None)
    cols = P(None, AXES)
    whole = P(AXES, None, None)
    weights = (rows, cols, rows, rows, rows, cols, rows, rows, cols)
    in_specs = (whole, rows, whole) + weights + (P(),) * 8
    out_specs = (whole, whole) + weights + (P(),) * 8
    return jax.shard_map(shards, mesh=mesh, in_specs=in_specs, out_specs=out_specs, check_vma=False)
```

```python
from functools import partial

import jax
import jax.numpy as jnp
from jax import lax
from jax.experimental import pallas as pl
from jax.experimental.pallas import tpu as pltpu
from jax.sharding import PartitionSpec as P

HEADS = 8
KV_HEADS = 2
HEAD_DIM = 128
M_HEADS = 24
M_HDIM = 64
STATE = 128
SPAN = 128
D_SSM = 1536
CONV_CH = 1792
QKV = (HEADS + 2 * KV_HEADS) * HEAD_DIM
PAIRS = M_HEADS // 2
QROWS = 256
REACH = 512

AXES = ("fsdp", "dp")
bf16 = jnp.bfloat16
f32 = jnp.float32
eps = 1e-06
rope_base = 100000000000.0
NEG = -1e30

NT = (((1,), (1,)), ((), ()))
TN = (((0,), (0,)), ((), ()))


def mm(left, right):
    return jnp.dot(left, right, preferred_element_type=f32)


def mm_nt(left, right):
    return lax.dot_general(left, right, NT, preferred_element_type=f32)


def mm_tn(left, right):
    return lax.dot_general(left, right, TN, preferred_element_type=f32)


def exact_mm(left, right):
    return jnp.dot(left, right, precision=lax.Precision.HIGHEST, preferred_element_type=f32)


def split_mm(value, selector):
    high = value.astype(bf16)
    low = (value - high.astype(f32)).astype(bf16)
    return mm(high, selector) + mm(low, selector)


def iota2(shape, axis):
    return lax.broadcasted_iota(jnp.int32, shape, axis)


def head_spread():
    rows = iota2((SPAN, D_SSM), 0)
    cols = iota2((SPAN, D_SSM), 1)
    return jnp.where(cols // M_HDIM == rows, 1.0, 0.0).astype(bf16)


def head_gather():
    rows = iota2((D_SSM, SPAN), 0)
    cols = iota2((D_SSM, SPAN), 1)
    return jnp.where(rows // M_HDIM == cols, 1.0, 0.0).astype(bf16)


def split_pair(block):
    lanes = iota2(block.shape, 1)
    zero = jnp.zeros_like(block)
    return jnp.concatenate(
        [jnp.where(lanes < M_HDIM, block, zero), jnp.where(lanes < M_HDIM, zero, block)], axis=0
    )


def block_terms(ld_ref, st_ref, spread):
    ld = ld_ref[...]
    st = st_ref[...]
    rows = iota2((SPAN, SPAN), 0)
    cols = iota2((SPAN, SPAN), 1)
    cum = exact_mm(jnp.where(rows >= cols, 1.0, 0.0), ld)
    cum_t = cum.T
    st_t = st.T
    doc = st[:, 127:128]
    prior = st[:, 126:127]
    last = st[:, 125:126]
    doc_row = st_t[127:128, :]
    carried = jnp.where(doc == prior, jnp.exp(cum), 0.0)
    gap = jnp.where(doc == last, jnp.exp(cum[SPAN - 1 : SPAN, :] - cum), 0.0)
    keep = jnp.where(last == prior, jnp.exp(cum[SPAN - 1 : SPAN, :]), 0.0)
    keep = keep[0:8, :]
    return (st, cum, cum_t, st_t, doc, doc_row, carried, gap, keep)


def scan_fwd_kernel(x_ref, b_ref, c_ref, ld_ref, st_ref, y_ref, states_ref, state):
    spread = head_spread()

    @pl.when(pl.program_id(0) == 0)
    def _():
        state[...] = jnp.zeros_like(state)

    st, cum, cum_t, st_t, doc, doc_row, carried, gap, keep = block_terms(ld_ref, st_ref, spread)
    rows = iota2((SPAN, SPAN), 0)
    cols = iota2((SPAN, SPAN), 1)
    bias = jnp.where((doc == doc_row) & (rows >= cols), 0.0, NEG)
    b_blk = b_ref[...]
    c_blk = c_ref[...]
    affinity = mm_nt(c_blk, b_blk)
    old = state[...]
    old_low = old.astype(bf16)
    states_ref[0] = old_low
    from_state = mm(c_blk, old_low) * split_mm(carried, spread)
    for pair in range(PAIRS):
        lo, hi = pair * SPAN, (pair + 1) * SPAN
        mats = []
        for h in (2 * pair, 2 * pair + 1):
            decay = jnp.exp(cum[:, h : h + 1] - cum_t[h : h + 1, :] + bias)
            mats.append((affinity * decay * st_t[h : h + 1, :]).astype(bf16))
        inside = mm(jnp.concatenate(mats, axis=1), split_pair(x_ref[:, lo:hi]))
        y_ref[:, lo:hi] = inside + from_state[:, lo:hi]
    tail = split_mm(gap * st, spread)
    pushed = (x_ref[...].astype(f32) * tail).astype(bf16)
    state[...] = old * split_mm(keep, spread)[0:1, :] + mm_tn(b_blk, pushed)


def scan_bwd_kernel(
    x_ref, b_ref, c_ref, ld_ref, st_ref, states_ref, dy_ref, skip_ref,
    dx_ref, dst_ref, dld_ref, dskip_ref, dstate, grow, gcol,
):
    spread = head_spread()
    gather = head_gather()

    @pl.when(pl.program_id(0) == 0)
    def _():
        dstate[...] = jnp.zeros_like(dstate)
        grow[...] = jnp.zeros_like(grow)
        gcol[...] = jnp.zeros_like(gcol)
        dskip_ref[...] = jnp.zeros_like(dskip_ref)

    st, cum, cum_t, st_t, doc, doc_row, carried, gap, keep = block_terms(ld_ref, st_ref, spread)
    rows = iota2((SPAN, SPAN), 0)
    cols = iota2((SPAN, SPAN), 1)
    bias = jnp.where((doc == doc_row) & (cols >= rows), 0.0, NEG)
    b_blk = b_ref[...]
    c_blk = c_ref[...]
    x_blk = x_ref[...]
    dy = dy_ref[...]
    dy_low = dy.astype(bf16)
    affinity = mm_nt(b_blk, c_blk)
    old_low = states_ref[0]
    d_new = dstate[...]
    d_new_low = d_new.astype(bf16)
    carried_wide = split_mm(carried, spread)
    tail_wide = split_mm(gap * st, spread)
    keep_wide = split_mm(keep, spread)[0:1, :]
    from_tail = mm(b_blk, d_new_low)
    d_aff = jnp.zeros((SPAN, SPAN), f32)
    for pair in range(PAIRS):
        lo, hi = pair * SPAN, (pair + 1) * SPAN
        d_mats = mm_nt(split_pair(x_blk[:, lo:hi]), dy_low[:, lo:hi])
        mats = []
        for which, h in enumerate((2 * pair, 2 * pair + 1)):
            step = st[:, h : h + 1]
            decay = jnp.exp(cum_t[h : h + 1, :] - cum[:, h : h + 1] + bias)
            scaled = affinity * decay
            mats.append((scaled * step).astype(bf16))
            d_mat = d_mats[which * SPAN : (which + 1) * SPAN, :]
            d_aff = d_aff + d_mat * decay * step
            products = d_mat * scaled
            gcol[:, h : h + 1] = jnp.sum(products, axis=1, keepdims=True)
            grow[h : h + 1, :] = jnp.sum(products * step, axis=0, keepdims=True)
        inside = mm(jnp.concatenate(mats, axis=1), split_pair(dy_low[:, lo:hi]))
        inside = inside + skip_ref[:, lo:hi] * dy[:, lo:hi]
        dx_ref[:, lo:hi] = inside + from_tail[:, lo:hi] * tail_wide[:, lo:hi]
    dskip_ref[0:1, :] += jnp.sum(dy * x_blk.astype(f32), axis=0, keepdims=True)
    flowing = dy * carried_wide
    flowing_low = flowing.astype(bf16)
    d_cum = split_mm(flowing * mm(c_blk, old_low), gather)
    d_tail = split_mm(x_blk.astype(f32) * from_tail, gather)
    moved = d_tail * gap * st
    d_keep = jnp.sum(d_new * old_low.astype(f32), axis=0, keepdims=True)
    d_keep = split_mm(jnp.broadcast_to(d_keep, (8, D_SSM)), gather) * keep
    at_end = jnp.sum(moved, axis=0, keepdims=True) + d_keep[0:1, :]
    d_cum = d_cum - moved + grow[...].T - gcol[...] * st
    d_cum = d_cum + jnp.where(rows == SPAN - 1, at_end, 0.0)
    dst_ref[...] = gcol[...] + d_tail * gap
    dld_ref[...] = exact_mm(jnp.where(cols >= rows, 1.0, 0.0), d_cum)
    d_aff_low = d_aff.astype(bf16)
    pushed = (x_blk.astype(f32) * tail_wide).astype(bf16)
    dx_ref[:, D_SSM + STATE :] = mm_tn(d_aff_low, b_blk) + mm_nt(flowing_low, old_low)
    dx_ref[:, D_SSM : D_SSM + STATE] = mm(d_aff_low, c_blk) + mm_nt(pushed, d_new_low)
    dstate[...] = d_new * keep_wide + mm_tn(c_blk, flowing_low)


def scan_fwd(act_low, ld, st):
    length = act_low.shape[0]
    blocks = length // SPAN
    return pl.pallas_call(
        scan_fwd_kernel,
        grid=(blocks,),
        in_specs=[
            pl.BlockSpec((SPAN, D_SSM), lambda i: (i, 0)),
            pl.BlockSpec((SPAN, STATE), lambda i: (i, D_SSM // STATE)),
            pl.BlockSpec((SPAN, STATE), lambda i: (i, D_SSM // STATE + 1)),
            pl.BlockSpec((SPAN, 128), lambda i: (i, 0)),
            pl.BlockSpec((SPAN, 128), lambda i: (i, 0)),
        ],
        out_specs=[
            pl.BlockSpec((SPAN, D_SSM), lambda i: (i, 0)),
            pl.BlockSpec((1, STATE, D_SSM), lambda i: (i, 0, 0)),
        ],
        out_shape=[
            jax.ShapeDtypeStruct((length, D_SSM), f32),
            jax.ShapeDtypeStruct((blocks, STATE, D_SSM), bf16),
        ],
        scratch_shapes=[pltpu.VMEM((STATE, D_SSM), f32)],
        compiler_params=pltpu.CompilerParams(vmem_limit_bytes=40 * 2**20),
    )(act_low, act_low, act_low, ld, st)


def scan_bwd(act_low, ld, st, states, dy, skip):
    length = act_low.shape[0]
    blocks = length // SPAN
    end = blocks - 1
    return pl.pallas_call(
        scan_bwd_kernel,
        grid=(blocks,),
        in_specs=[
            pl.BlockSpec((SPAN, D_SSM), lambda i: (end - i, 0)),
            pl.BlockSpec((SPAN, STATE), lambda i: (end - i, D_SSM // STATE)),
            pl.BlockSpec((SPAN, STATE), lambda i: (end - i, D_SSM // STATE + 1)),
            pl.BlockSpec((SPAN, 128), lambda i: (end - i, 0)),
            pl.BlockSpec((SPAN, 128), lambda i: (end - i, 0)),
            pl.BlockSpec((1, STATE, D_SSM), lambda i: (end - i, 0, 0)),
            pl.BlockSpec((SPAN, D_SSM), lambda i: (end - i, 0)),
            pl.BlockSpec((1, D_SSM), lambda i: (0, 0)),
        ],
        out_specs=[
            pl.BlockSpec((SPAN, CONV_CH), lambda i: (end - i, 0)),
            pl.BlockSpec((SPAN, 128), lambda i: (end - i, 0)),
            pl.BlockSpec((SPAN, 128), lambda i: (end - i, 0)),
            pl.BlockSpec((8, D_SSM), lambda i: (0, 0)),
        ],
        out_shape=[
            jax.ShapeDtypeStruct((length, CONV_CH), f32),
            jax.ShapeDtypeStruct((length, 128), f32),
            jax.ShapeDtypeStruct((length, 128), f32),
            jax.ShapeDtypeStruct((8, D_SSM), f32),
        ],
        scratch_shapes=[
            pltpu.VMEM((STATE, D_SSM), f32),
            pltpu.VMEM((SPAN, SPAN), f32),
            pltpu.VMEM((SPAN, SPAN), f32),
        ],
        compiler_params=pltpu.CompilerParams(vmem_limit_bytes=40 * 2**20),
    )(act_low, act_low, act_low, ld, st, states, dy, skip)


def key_span(block):
    return max(0, block * QROWS - REACH), (block + 1) * QROWS


def fill_bias(doc_col_ref, doc_row_ref, bias, blocks):
    for block in range(blocks):
        k0, k1 = key_span(block)
        q0, q1 = block * QROWS, (block + 1) * QROWS
        shape = (k1 - k0, QROWS)
        allowed = (doc_col_ref[k0:k1, :] == doc_row_ref[:, q0:q1]) & (
            iota2(shape, 0) + k0 <= iota2(shape, 1) + q0
        )
        bias[block, 0 : k1 - k0, :] = jnp.where(allowed, 0.0, NEG)


def attend_fwd_kernel(q_ref, k_ref, v_ref, doc_col_ref, doc_row_ref, out_ref, lse_ref, bias):
    blocks = q_ref.shape[0] // QROWS

    @pl.when(pl.program_id(0) == 0)
    def _():
        fill_bias(doc_col_ref, doc_row_ref, bias, blocks)

    for block in range(blocks):
        k0, k1 = key_span(block)
        q0, q1 = block * QROWS, (block + 1) * QROWS
        scores = mm_nt(k_ref[k0:k1, :], q_ref[q0:q1, :]) * HEAD_DIM ** (-0.5)
        scores = scores + bias[block, 0 : k1 - k0, :]
        top = jnp.max(scores, axis=0, keepdims=True)
        exponent = jnp.exp(scores - top)
        total = jnp.sum(exponent, axis=0, keepdims=True)
        probability = (exponent * (1.0 / total)).astype(bf16)
        out_ref[q0:q1, :] = mm_tn(v_ref[k0:k1, :], probability).T.astype(bf16)
        lse_ref[0, :, q0:q1] = top + jnp.log(total)


def attend_bwd_kernel(
    q_ref, k_ref, v_ref, do_ref, lse_ref, doc_col_ref, doc_row_ref, dq_ref, dk_ref, dv_ref, bias
):
    blocks = q_ref.shape[0] // QROWS

    @pl.when((pl.program_id(0) == 0) & (pl.program_id(1) == 0))
    def _():
        fill_bias(doc_col_ref, doc_row_ref, bias, blocks)

    @pl.when(pl.program_id(1) == 0)
    def _():
        dk_ref[...] = jnp.zeros_like(dk_ref)
        dv_ref[...] = jnp.zeros_like(dv_ref)

    for block in range(blocks):
        k0, k1 = key_span(block)
        q0, q1 = block * QROWS, (block + 1) * QROWS
        query = q_ref[q0:q1, :]
        key = k_ref[k0:k1, :]
        d_out = do_ref[q0:q1, :].astype(bf16)
        scores = mm_nt(key, query) * HEAD_DIM ** (-0.5) + bias[block, 0 : k1 - k0, :]
        probability = jnp.exp(scores - lse_ref[0, :, q0:q1])
        dv_ref[k0:k1, :] += mm(probability.astype(bf16), d_out)
        d_prob = mm_nt(v_ref[k0:k1, :], d_out)
        delta = jnp.sum(probability * d_prob, axis=0, keepdims=True)
        d_scores = (probability * (d_prob - delta) * HEAD_DIM ** (-0.5)).astype(bf16)
        dk_ref[k0:k1, :] += mm(d_scores, query)
        dq_ref[q0:q1, :] = mm_tn(key, d_scores).T


def attend_fwd(query, key, value, doc_col, doc_row):
    length = query.shape[0]
    group = HEADS // KV_HEADS
    blocks = length // QROWS
    return pl.pallas_call(
        attend_fwd_kernel,
        grid=(HEADS,),
        in_specs=[
            pl.BlockSpec((length, HEAD_DIM), lambda h: (0, h)),
            pl.BlockSpec((length, HEAD_DIM), lambda h: (0, h // group)),
            pl.BlockSpec((length, HEAD_DIM), lambda h: (0, h // group)),
            pl.BlockSpec((length, 1), lambda h: (0, 0)),
            pl.BlockSpec((1, length), lambda h: (0, 0)),
        ],
        out_specs=[
            pl.BlockSpec((length, HEAD_DIM), lambda h: (0, h)),
            pl.BlockSpec((1, 1, length), lambda h: (h, 0, 0)),
        ],
        out_shape=[
            jax.ShapeDtypeStruct((length, HEADS * HEAD_DIM), bf16),
            jax.ShapeDtypeStruct((HEADS, 1, length), f32),
        ],
        scratch_shapes=[pltpu.VMEM((blocks, QROWS + REACH, QROWS), f32)],
        compiler_params=pltpu.CompilerParams(vmem_limit_bytes=40 * 2**20),
    )(query, key, value, doc_col, doc_row)


def attend_bwd(query, key, value, d_out, lse, doc_col, doc_row):
    length = query.shape[0]
    group = HEADS // KV_HEADS
    blocks = length // QROWS
    per_query = pl.BlockSpec((length, HEAD_DIM), lambda g, r: (0, g * group + r))
    per_key = pl.BlockSpec((length, HEAD_DIM), lambda g, r: (0, g))
    return pl.pallas_call(
        attend_bwd_kernel,
        grid=(KV_HEADS, group),
        in_specs=[
            per_query,
            per_key,
            per_key,
            per_query,
            pl.BlockSpec((1, 1, length), lambda g, r: (g * group + r, 0, 0)),
            pl.BlockSpec((length, 1), lambda g, r: (0, 0)),
            pl.BlockSpec((1, length), lambda g, r: (0, 0)),
        ],
        out_specs=[per_query, per_key, per_key],
        out_shape=[
            jax.ShapeDtypeStruct((length, HEADS * HEAD_DIM), f32),
            jax.ShapeDtypeStruct((length, KV_HEADS * HEAD_DIM), f32),
            jax.ShapeDtypeStruct((length, KV_HEADS * HEAD_DIM), f32),
        ],
        scratch_shapes=[pltpu.VMEM((blocks, QROWS + REACH, QROWS), f32)],
        compiler_params=pltpu.CompilerParams(vmem_limit_bytes=40 * 2**20),
    )(query, key, value, d_out, lse, doc_col, doc_row)


LANES = 128
CONV_BLOCKS = CONV_CH // LANES


def conv_shifts(values, mask_ref, taps):
    shifts = [values]
    for offset in range(1, taps):
        allowed = jnp.broadcast_to(mask_ref[:, offset : offset + 1], values.shape)
        shifts.append(jnp.where(allowed > 0.0, pltpu.roll(values, offset, 0), 0.0))
    return shifts


def conv_sum(shifts, weight_ref, bias_ref):
    total = bias_ref[...]
    for offset, shifted in enumerate(shifts):
        total = total + weight_ref[offset : offset + 1, :] * shifted
    return total


def conv_fwd_kernel(x_ref, mask_ref, weight_ref, bias_ref, act_ref):
    total = conv_sum(conv_shifts(x_ref[...], mask_ref, weight_ref.shape[0]), weight_ref, bias_ref)
    act_ref[...] = (total * jax.nn.sigmoid(total)).astype(bf16)


def conv_bwd_kernel(
    x_ref, d_act_ref, d_raw_ref, mask_ref, weight_ref, bias_ref, out_ref, small_ref
):
    step = pl.program_id(0)
    length = x_ref.shape[0]

    @pl.when(step == CONV_BLOCKS)
    def _():
        out_ref[...] = d_raw_ref[...]

    @pl.when(step < CONV_BLOCKS)
    def _():
        shifts = conv_shifts(x_ref[...], mask_ref, weight_ref.shape[0])
        total = conv_sum(shifts, weight_ref, bias_ref)
        gate = jax.nn.sigmoid(total)
        d_total = d_act_ref[...] * (gate * (1.0 + total * (1.0 - gate)))
        small_ref[...] = jnp.zeros_like(small_ref)
        small_ref[0:1, :] = jnp.sum(d_total, axis=0, keepdims=True)
        d_in = weight_ref[0:1, :] * d_total
        for offset, shifted in enumerate(shifts):
            small_ref[offset + 1 : offset + 2, :] = jnp.sum(d_total * shifted, axis=0, keepdims=True)
            if offset:
                allowed = jnp.broadcast_to(mask_ref[:, offset : offset + 1], d_total.shape)
                masked = jnp.where(allowed > 0.0, d_total, 0.0)
                later = pltpu.roll(masked, length - offset, 0)
                d_in = d_in + weight_ref[offset : offset + 1, :] * later
        out_ref[...] = d_in.astype(bf16)


def conv_fwd(proj, first, masks, weight, bias):
    length, taps = masks.shape
    return pl.pallas_call(
        conv_fwd_kernel,
        grid=(CONV_BLOCKS,),
        in_specs=[
            pl.BlockSpec((length, LANES), lambda i: (0, first + i)),
            pl.BlockSpec((length, taps), lambda i: (0, 0)),
            pl.BlockSpec((taps, LANES), lambda i: (0, i)),
            pl.BlockSpec((1, LANES), lambda i: (0, i)),
        ],
        out_specs=pl.BlockSpec((length, LANES), lambda i: (0, i)),
        out_shape=jax.ShapeDtypeStruct((length, CONV_CH), bf16),
        compiler_params=pltpu.CompilerParams(vmem_limit_bytes=40 * 2**20),
    )(proj, masks, weight, bias)


def conv_bwd(proj, first, d_act, d_raw, masks, weight, bias):
    length, taps = masks.shape
    end = CONV_BLOCKS - 1
    return pl.pallas_call(
        conv_bwd_kernel,
        grid=(CONV_BLOCKS + 1,),
        in_specs=[
            pl.BlockSpec((length, LANES), lambda i: (0, first + jnp.minimum(i, end))),
            pl.BlockSpec((length, LANES), lambda i: (0, jnp.minimum(i, end))),
            pl.BlockSpec((length, LANES), lambda i: (0, 0)),
            pl.BlockSpec((length, taps), lambda i: (0, 0)),
            pl.BlockSpec((taps, LANES), lambda i: (0, jnp.minimum(i, end))),
            pl.BlockSpec((1, LANES), lambda i: (0, jnp.minimum(i, end))),
        ],
        out_specs=[
            pl.BlockSpec((length, LANES), lambda i: (0, i)),
            pl.BlockSpec((8, LANES), lambda i: (0, jnp.minimum(i, end))),
        ],
        out_shape=[
            jax.ShapeDtypeStruct((length, CONV_CH + LANES), bf16),
            jax.ShapeDtypeStruct((8, CONV_CH), f32),
        ],
        compiler_params=pltpu.CompilerParams(vmem_limit_bytes=40 * 2**20),
    )(proj, d_act, d_raw, masks, weight, bias)


def units_bwd_kernel(cot_ref, down_ref, both_ref, out_ref):
    units = down_ref.shape[1]
    d_hidden = mm(cot_ref[...], down_ref[...])
    gate = both_ref[:, :units]
    sigmoid = jax.nn.sigmoid(gate)
    slope = sigmoid * (1.0 + gate * (1.0 - sigmoid))
    out_ref[:, :units] = (d_hidden * both_ref[:, units:] * slope).astype(bf16)
    out_ref[:, units:] = (d_hidden * (gate * sigmoid)).astype(bf16)


def units_bwd(cot, weights, both):
    length, width = cot.shape
    units = both.shape[1] // 2
    rows = 128
    return pl.pallas_call(
        units_bwd_kernel,
        grid=(length // rows,),
        in_specs=[
            pl.BlockSpec((rows, width), lambda i: (i, 0)),
            pl.BlockSpec((width, units), lambda i: (0, 0)),
            pl.BlockSpec((rows, 2 * units), lambda i: (i, 0)),
        ],
        out_specs=pl.BlockSpec((rows, 2 * units), lambda i: (i, 0)),
        out_shape=jax.ShapeDtypeStruct((length, 2 * units), bf16),
        compiler_params=pltpu.CompilerParams(vmem_limit_bytes=40 * 2**20),
    )(cot, weights, both)


def inv_norm(values):
    return lax.rsqrt(jnp.mean(values * values, axis=-1, keepdims=True) + eps)


def norm_back(normed_grad, gain, values, inv, tie=lambda mean: mean):
    unit = values * inv
    scaled = normed_grad * gain
    back = inv * (scaled - unit * tie(jnp.mean(scaled * unit, axis=-1, keepdims=True)))
    return back, jnp.sum(normed_grad * unit, axis=0)


def angles(length):
    half_dim = HEAD_DIM // 2
    frequency = rope_base ** (-jnp.arange(half_dim, dtype=f32) / half_dim)
    table = jnp.arange(length).astype(f32)[:, None] * frequency[None, :]
    return jnp.cos(table), jnp.sin(table)


def turn(values, cosine, sine):
    length, width = values.shape
    heads = values.reshape(length, width // HEAD_DIM, HEAD_DIM)
    front, back = jnp.split(heads, 2, axis=-1)
    cosine, sine = cosine[:, None, :], sine[:, None, :]
    turned = jnp.concatenate([front * cosine - back * sine, back * cosine + front * sine], axis=-1)
    return turned.reshape(length, width)


def silu_slope(values):
    gate = jax.nn.sigmoid(values)
    return gate * (1.0 + values * (1.0 - gate))


def same_doc(doc_ids, offset):
    earlier = jnp.pad(doc_ids, (offset, 0), constant_values=-1)[: doc_ids.shape[0]]
    return (earlier == doc_ids)[:, None]


def flip(values, bit):
    places = lax.axis_size(AXES)
    return lax.ppermute(values, AXES, [(i, i ^ bit) for i in range(places)])


def add(left, right):
    return (left.astype(f32) + right.astype(f32)).astype(bf16)


def at(values, index, axis):
    return lax.dynamic_index_in_dim(values, index, axis, keepdims=False)


def scatter_steps(grads):
    dp = lax.axis_size("dp")
    chips = lax.axis_size("fsdp") // 2
    if dp != 2 or chips < 4:
        return lax.psum_scatter(grads, AXES, scatter_dimension=0, tiled=True).astype(f32)
    rows, width = grads.shape
    held = rows // (4 * chips)
    place = lax.axis_index("fsdp")
    core, y, z, x = place % 2, (place // 2) % 2, place // 4, lax.axis_index("dp")
    blocks = grads.reshape(chips, 2, 2 * held, width)
    shape = (chips // 2, 2, 2, held, width)
    own = at(blocks, core, 1).reshape(shape)
    other = (yield flip(at(blocks, 1 - core, 1), 2)).reshape(shape)

    def pick(row, col):
        zero = jnp.zeros((), place.dtype)
        start, size = (zero, row, col, zero, zero), (chips // 2, 1, 1, held, width)
        return add(lax.dynamic_slice(own, start, size), lax.dynamic_slice(other, start, size))[:, 0, 0]

    def along(first):
        return jnp.stack(
            [
                pick(jnp.where(core == 0, second, first), jnp.where(core == 0, first, second))
                for second in jnp.arange(2, dtype=place.dtype)
            ]
        )

    near = jnp.where(core == 0, x, y)
    far = jnp.where(core == 0, y, x)
    places = 4 * chips
    crossing = [(i, i ^ (4 if i & 2 else 1)) for i in range(places)]
    back = [(i, i ^ (1 if i & 2 else 4)) for i in range(places)]
    sent, own = along(1 - near), along(near)
    other = yield lax.ppermute(sent, AXES, crossing)
    sent = add(at(own, 1 - far, 0), at(other, 1 - far, 0))
    own = add(at(own, far, 0), at(other, far, 0))
    other = yield lax.ppermute(sent, AXES, back)
    level = 1
    while level < chips // 2:
        shape = (-1, 2, held, width)
        mine = (z // level) % 2
        own, other = own.reshape(shape), other.reshape(shape)
        sent = add(at(own, 1 - mine, 1), at(other, 1 - mine, 1))
        own = add(at(own, mine, 1), at(other, mine, 1))
        other = yield flip(sent, 8 * level)
        level *= 2
    return (own.astype(f32) + other.astype(f32)).reshape(held, width)


class Sums:
    def __init__(self):
        self.flying, self.sums = {}, {}

    def move(self, name, steps, value):
        try:
            self.flying[name] = (steps, steps.send(value))
        except StopIteration as stop:
            self.sums[name] = stop.value
            self.flying.pop(name, None)

    def start(self, name, grads):
        self.move(name, scatter_steps(grads.astype(bf16)), None)

    def step(self, anchor, *names):
        names = [name for name in (names or tuple(self.flying)) if name in self.flying]
        anchor, arrived = lax.optimization_barrier(
            (anchor, tuple(self.flying[name][1] for name in names))
        )
        for name, value in zip(names, arrived):
            self.move(name, self.flying[name][0], value)
        return anchor


def sum_everywhere(values):
    bit = 1
    while bit < lax.axis_size(AXES):
        values = values + flip(values, bit)
        bit *= 2
    return values


def gather(parts):
    return lax.all_gather(jnp.concatenate(parts, axis=1), AXES, axis=0, tiled=True)


def shards(
    tokens, segments, cotangent, w_in, w_out, w_query, w_key, w_value, w_attn_out, w_gate, w_up,
    w_down, norm_in, conv_weight, conv_bias, dt_bias, a_log, skip_gain, norm_gated, norm_mid,
):
    length = tokens.shape[1]
    blocks = length // SPAN
    conv_end = D_SSM + CONV_CH
    rows_held = w_in.shape[0]
    dt_pad = jnp.zeros((rows_held, 128 - M_HEADS), bf16)
    w_first = gather(
        (w_in[:, :D_SSM], w_query, w_key, w_value, w_in[:, D_SSM:conv_end], w_in[:, conv_end:], dt_pad)
    )
    w_later = gather((w_down.T, w_gate, w_up, w_attn_out.T, w_out.T))
    fourth_end = w_down.shape[0]
    third_end = fourth_end + 2 * w_gate.shape[1]
    w_fourth = w_later[:, :fourth_end]
    w_third = w_later[:, fourth_end:third_end]
    w_second = w_later[:, third_end:]

    stream = tokens[0].astype(f32)
    doc_ids = segments[0]
    cot = cotangent[0]

    inv_in = inv_norm(stream)
    normed = (stream * inv_in * norm_in).astype(bf16)
    proj = mm(normed, w_first)
    z_gate = proj[:, :D_SSM]
    q_at, k_at, v_at = D_SSM, D_SSM + HEADS * HEAD_DIM, D_SSM + (HEADS + KV_HEADS) * HEAD_DIM
    conv_at = D_SSM + QKV
    dt_at = conv_at + CONV_CH
    cosine, sine = angles(length)
    query = turn(proj[:, q_at:k_at], cosine, sine).astype(bf16)
    key = turn(proj[:, k_at:v_at], cosine, sine).astype(bf16)
    value = proj[:, v_at:conv_at].astype(bf16)
    doc_float = doc_ids.astype(f32)
    doc_col, doc_row = doc_float[:, None], doc_float[None, :]
    attended, lse = attend_fwd(query, key, value, doc_col, doc_row)

    taps = conv_weight.shape[0]
    masks = jnp.concatenate([same_doc(doc_ids, offset) for offset in range(taps)], axis=1).astype(f32)
    conv_bias_row = conv_bias[None, :]
    act_low = conv_fwd(proj, conv_at // LANES, masks, conv_weight, conv_bias_row)
    x_heads = act_low[:, :D_SSM]
    raw = proj[:, dt_at : dt_at + M_HEADS] + dt_bias
    step_size = jax.nn.softplus(raw)
    log_decay = -step_size * jnp.exp(a_log)
    doc_blocks = doc_float.reshape(blocks, SPAN)
    last = doc_blocks[:, -1]
    prior = jnp.concatenate([jnp.full((1,), -1.0, f32), last[:-1]])
    wide_last = jnp.repeat(last, SPAN)[:, None]
    wide_prior = jnp.repeat(prior, SPAN)[:, None]
    ld = jnp.pad(log_decay, ((0, 0), (0, 128 - M_HEADS)))
    st = jnp.concatenate(
        [step_size, jnp.zeros((length, 125 - M_HEADS), f32), wide_last, wide_prior, doc_col], axis=1
    )
    scanned, states = scan_fwd(act_low, ld, st)
    skip_wide = jnp.repeat(skip_gain, M_HDIM)[None, :]
    ssm_out = scanned + skip_wide * x_heads.astype(f32)
    mixed_in = ssm_out * jax.nn.silu(z_gate)
    inv_gated = inv_norm(mixed_in)
    gated = (mixed_in * inv_gated * norm_gated).astype(bf16)
    branches = jnp.concatenate([attended, gated], axis=1)
    resid = stream + mm_nt(branches, w_second)
    inv_mid = inv_norm(resid)
    mid_in = (resid * inv_mid * norm_mid).astype(bf16)
    both = mm(mid_in, w_third)
    hidden_units = both.shape[1] // 2
    gate, up = both[:, :hidden_units], both[:, hidden_units:]
    hidden = (jax.nn.silu(gate) * up).astype(bf16)
    mixed = (resid + mm_nt(hidden, w_fourth)).astype(bf16)

    sums = Sums()
    sums.start("fourth", mm_tn(cot, hidden))
    d_both = units_bwd(cot, w_later, both)
    d_both = sums.step(d_both)
    sums.start("third", mm_tn(mid_in, d_both))
    d_mid = mm_nt(d_both, w_third)
    back, g_norm_mid = norm_back(d_mid, norm_mid, resid, inv_mid, sums.step)
    d_resid = cot.astype(f32) + back
    d_resid_low = d_resid.astype(bf16)
    sums.start("second", mm_tn(d_resid_low, branches))
    d_branches = sums.step(mm(d_resid_low, w_second), "fourth", "second")
    attn_width = HEADS * HEAD_DIM
    d_query, d_key, d_value = attend_bwd(
        query, key, value, d_branches[:, :attn_width], lse, doc_col, doc_row
    )
    d_query, d_branches = sums.step((d_query, d_branches))
    d_mixed_in, g_norm_gated = norm_back(d_branches[:, attn_width:], norm_gated, mixed_in, inv_gated)
    d_ssm = d_mixed_in * jax.nn.silu(z_gate)
    d_first = jnp.concatenate(
        [
            (d_mixed_in * ssm_out * silu_slope(z_gate)).astype(bf16),
            turn(d_query, cosine, -sine).astype(bf16),
            turn(d_key, cosine, -sine).astype(bf16),
            d_value.astype(bf16),
        ],
        axis=1,
    )
    sums.start("first", mm_tn(normed, d_first))
    d_act, d_st, d_ld, g_skip_wide = scan_bwd(act_low, ld, st, states, d_ssm, skip_wide)
    g_skip = jnp.sum(g_skip_wide[0].reshape(M_HEADS, M_HDIM), axis=1)
    d_st = sums.step(d_st)
    d_ld = d_ld[:, :M_HEADS]
    d_step = d_st[:, :M_HEADS] - d_ld * jnp.exp(a_log)
    g_a_log = jnp.sum(d_ld * log_decay, axis=0)
    d_raw = d_step * jax.nn.sigmoid(raw)
    g_dt_bias = jnp.sum(d_raw, axis=0)
    d_raw_low = jnp.pad(d_raw.astype(bf16), ((0, 0), (0, LANES - M_HEADS)))
    d_last, g_conv = conv_bwd(
        proj, conv_at // LANES, d_act, d_raw_low, masks, conv_weight, conv_bias_row
    )
    g_conv_bias, g_conv_weight = g_conv[0], g_conv[1 : taps + 1]
    d_last = sums.step(d_last)
    sums.start("last", mm_tn(normed, d_last))
    d_normed = mm_nt(d_first, w_first[:, :conv_at])
    d_last = sums.step(d_last)
    d_normed = d_normed + mm_nt(d_last, w_first[:, conv_at:])
    back, g_norm_in = norm_back(d_normed, norm_in, stream, inv_in, sums.step)
    grad_tokens = d_resid + back
    while sums.flying:
        sums.step(())
    sum_first, sum_last = sums.sums["first"], sums.sums["last"]
    sum_second, sum_third, sum_fourth = sums.sums["second"], sums.sums["third"], sums.sums["fourth"]

    small = (
        g_norm_in, g_conv_weight, g_conv_bias, g_dt_bias, g_a_log, g_skip, g_norm_gated, g_norm_mid
    )
    flat = jnp.concatenate([member.reshape(-1) for member in small])
    flat = sum_everywhere(jnp.pad(flat, (0, -flat.shape[0] % 1024)).reshape(-1, 128)).reshape(-1)
    totals, at = [], 0
    for member in small:
        totals.append(flat[at : at + member.size].reshape(member.shape))
        at += member.size

    g_w_in = jnp.concatenate([sum_first[:, :D_SSM], sum_last[:, : CONV_CH + M_HEADS]], axis=1)
    return (
        mixed[None],
        grad_tokens[None],
        g_w_in,
        sum_second[:, attn_width:].T,
        sum_first[:, q_at:k_at],
        sum_first[:, k_at:v_at],
        sum_first[:, v_at:],
        sum_second[:, :attn_width].T,
        sum_third[:, :hidden_units],
        sum_third[:, hidden_units:],
        sum_fourth.T,
    ) + tuple(totals)


def solution(mesh):
    rows = P(AXES, None)
    cols = P(None, AXES)
    whole = P(AXES, None, None)
    weights = (rows, cols, rows, rows, rows, cols, rows, rows, cols)
    in_specs = (whole, rows, whole) + weights + (P(),) * 8
    out_specs = (whole, whole) + weights + (P(),) * 8
    return jax.shard_map(shards, mesh=mesh, in_specs=in_specs, out_specs=out_specs, check_vma=False)
```
